32 devices in a mesh: space: 4 (over y, core), angle: 8 (over z, x).
Axes of the slice: x: 2, y: 2, z: 4, core: 2. Of those that a mesh axis runs over, the one named last changes fastest.
Arguments:
- image: float32 [16384, 128], P(('space', 'angle')), may hold values from 0 to 1
- tiles: bfloat16 [4, 768, 128, 128], P('space', 'angle'), may hold values from -0.109375 to 0.109375
- tile_slot: int32 [4, 768], P('space', 'angle'), may hold values from 0 to 7, as said below
- tile_block: int32 [4, 768], P('space', 'angle'), may hold values from 0 to 31
- slot_ray: int32 [4, 64], P('space', 'angle'), may hold values from 0 to 15, as said below
- sinogram: bfloat16 [8, 16, 128, 128], P('angle', 'space'), may hold values from -4 to 4
- weights: bfloat16 [8, 16, 128, 128], P('angle', 'space'), may hold values from 0.29882812 to 3
Outputs:
- volume: float32 [16384, 128], P(('space', 'angle'))
- residual: bfloat16 [8, 16, 128, 128], P('angle', 'space')
The draws below stay inside these ranges and needn't reach their ends.
Inputs may be any that keep to these rules, and one draw needn't show every extreme that they name: `tile_slot`: every slot of a device is fed by at least one of its tiles. `slot_ray`: the 8 entries of one device are distinct; of the ray blocks k * 4 to (k + 1) * 4 - 1 of its angle group, one device lists at most 2, and in every angle group some k is listed 2 times by every device of the group.
All inputs are finite; a program needn't handle non-finite values.
Results may differ from the reference program's by a relative error of at most 0.025.
Values may be sent and summed in bfloat16 or wider, within the bound.
A program may use at most 64 MiB of HBM per device.

```python
import math
import jax
import jax.numpy as jnp
from jax import lax

TILE = 128
SLICES = 128
TILES_DEV = 96
BLOCKS = 32
SLOTS = 8
CAP = 2
OWN = 4
ITERS = 2
RAYS = 16
IMAGE_ROWS = 16384
N_SPACE = 4
N_ANGLE = 8


def draw_tile_slot(key, part):

    def per_device(device):
        ordering = jax.random.permutation(jax.random.fold_in(key, device + 3), TILES_DEV)
        return (ordering % SLOTS).astype(jnp.int32)
    listed = jax.vmap(per_device)(jnp.arange(N_SPACE * N_ANGLE, dtype=jnp.int32))
    return listed.reshape(N_SPACE, N_ANGLE * TILES_DEV)


def draw_slot_ray(key, part):
    hot_owner = jax.random.randint(jax.random.fold_in(key, 7), (N_ANGLE,), 0, N_SPACE)

    def per_device(device):
        angle_group = device % N_ANGLE
        device_key = jax.random.fold_in(key, device + 11)
        first_key, second_key, third_key = jax.random.split(device_key, 3)
        seat_order = jax.random.permutation(first_key, (N_SPACE - 1) * CAP)[:SLOTS - CAP]
        other_owner = seat_order // CAP
        counts_other = jnp.sum((other_owner[:, None] == jnp.arange(N_SPACE - 1)[None, :]).astype(jnp.int32), axis=0)
        owners = jnp.arange(N_SPACE)
        hot_here = hot_owner[angle_group]
        shifted = jnp.clip(owners - (owners > hot_here).astype(jnp.int32), 0, N_SPACE - 2)
        counts = jnp.where(owners == hot_here, CAP, counts_other[shifted])
        owner_keys = jax.random.split(second_key, N_SPACE)

        def choose(owner_key):
            return jax.random.permutation(owner_key, OWN)[:CAP]
        chosen = jax.vmap(choose)(owner_keys)
        seat_rank = jnp.arange(CAP)
        is_live = seat_rank[None, :] < counts[:, None]
        ray_list = owners[:, None] * OWN + chosen
        sort_keys = jnp.where(is_live, owners[:, None] * CAP + seat_rank[None, :], N_SPACE * CAP + 1)
        ordering = jnp.argsort(sort_keys.reshape(-1), stable=True)[:SLOTS]
        picked = ray_list.reshape(-1)[ordering]
        shuffle = jax.random.permutation(third_key, SLOTS)
        return picked[shuffle].astype(jnp.int32)
    listed = jax.vmap(per_device)(jnp.arange(N_SPACE * N_ANGLE, dtype=jnp.int32))
    return listed.reshape(N_SPACE, N_ANGLE * SLOTS)


def set_ends(result, stream_key, least, top_value):
    index_at = [jax.random.randint(jax.random.fold_in(stream_key, axis), (), 0, length) for axis, length in enumerate(result.shape)]
    longest = result.shape.index(max(result.shape))
    next_to = index_at[:longest] + [(index_at[longest] + 1) % result.shape[longest]] + index_at[longest + 1:]
    return result.at[tuple(index_at)].set(least).at[tuple(next_to)].set(top_value)


def block_scale(rng, extent, cuts, low, largest):
    factor_of = 1.0
    for position, parts in cuts:
        draws = jax.random.uniform(jax.random.fold_in(jax.random.fold_in(rng, 6), position), (parts,), jnp.float32, low / len(cuts), largest / len(cuts))
        factor_of = factor_of * jnp.repeat(jnp.exp(draws), extent[position] // parts).reshape((-1,) + (1,) * (len(extent) - 1 - position))
    return factor_of


def noise(rng, extent, deviation, reach, pieces=(), kind=jnp.bfloat16):
    factor_of = block_scale(rng, extent, pieces, -0.22, 0.18) if pieces else 1.0
    drawn = jax.random.normal(rng, extent, jnp.float32) * deviation * factor_of
    return jnp.minimum(jnp.maximum(drawn, -reach), reach).astype(kind)


def setup_inputs(seed: int = 0) -> dict:
    key_of = jax.random.split(jax.random.key(seed), 8)
    return {
        "image": jnp.clip(1.0 * jax.random.uniform(key_of[0], (IMAGE_ROWS, SLICES), jnp.float32) ** block_scale(key_of[0], (IMAGE_ROWS, SLICES), ((0, 32),), -0.2, 0.2), 0.0, 1.0),
        "tiles": noise(key_of[1], (N_SPACE, N_ANGLE * TILES_DEV, TILE, TILE), (TILE * TILES_DEV * N_SPACE // RAYS) ** -0.5, 0.109375, ((0, 4), (1, 8))),
        "tile_slot": draw_tile_slot(jax.random.fold_in(key_of[7], 71), 0),
        "tile_block": set_ends(jax.random.randint(key_of[3], (N_SPACE, N_ANGLE * TILES_DEV), 0, BLOCKS), jax.random.fold_in(key_of[3], 1), 0, BLOCKS - 1).astype(jnp.int32),
        "slot_ray": draw_slot_ray(jax.random.fold_in(key_of[7], 71), 0),
        "sinogram": noise(key_of[5], (N_ANGLE, RAYS, TILE, SLICES), 0.6, 4.0, ((0, 8), (1, 4))),
        "weights": jnp.clip(jnp.exp(math.log(3.0) - 2.306499 * jax.random.uniform(key_of[6], (N_ANGLE, RAYS, TILE, SLICES), jnp.float32) ** block_scale(key_of[6], (N_ANGLE, RAYS, TILE, SLICES), ((0, 8), (1, 4)), -0.2, 0.2)), 0.29882812, 3.0).astype(jnp.bfloat16),
    }


def reference(image, tiles, tile_slot, tile_block, slot_ray, sinogram, weights):
    tile_sets = tiles.reshape(N_SPACE, N_ANGLE, TILES_DEV, TILE, TILE)
    slot_sets = tile_slot.reshape(N_SPACE, N_ANGLE, TILES_DEV).astype(jnp.int32)
    block_sets = tile_block.reshape(N_SPACE, N_ANGLE, TILES_DEV).astype(jnp.int32)
    ray_sets = slot_ray.reshape(N_SPACE, N_ANGLE, SLOTS).astype(jnp.int32)
    step_size = 0.2 * math.sqrt(BLOCKS / (N_ANGLE * OWN))
    observed = sinogram.astype(jnp.float32)
    scales = weights.astype(jnp.float32)
    spaces = jnp.arange(N_SPACE, dtype=jnp.int32)
    angles = jnp.arange(N_ANGLE, dtype=jnp.int32)
    current = image
    residual = None
    for iteration in range(ITERS):
        pixels = current.astype(jnp.bfloat16).reshape(N_SPACE, BLOCKS, TILE, SLICES)

        def project(angle_group):

            def add_domain(running, space_index):
                tile_mats = tile_sets[space_index, angle_group].astype(jnp.float32)
                picked = pixels[space_index][block_sets[space_index, angle_group]].astype(jnp.float32)
                products = jnp.einsum('tij,tjk->tik', tile_mats, picked)
                partial_value = jax.ops.segment_sum(products, slot_sets[space_index, angle_group], num_segments=SLOTS)
                partial_value = lax.optimization_barrier(partial_value.astype(jnp.bfloat16)).astype(jnp.float32)
                running = running.at[ray_sets[space_index, angle_group]].add(partial_value)
                return (running, None)
            running, _ = lax.scan(add_domain, jnp.zeros((RAYS, TILE, SLICES), jnp.float32), spaces)
            return running
        ray_sums = lax.map(project, angles)
        residual = (scales * (ray_sums - observed)).astype(jnp.bfloat16)

        def backproject(space_index):

            def add_angle(running, angle_group):
                tile_mats = tile_sets[space_index, angle_group].astype(jnp.float32)
                slot_res = residual[angle_group][ray_sets[space_index, angle_group]]
                tile_res = slot_res[slot_sets[space_index, angle_group]].astype(jnp.float32)
                back_terms = jnp.einsum('tji,tjk->tik', tile_mats, tile_res)
                block_part = jax.ops.segment_sum(back_terms, block_sets[space_index, angle_group], num_segments=BLOCKS)
                block_part = lax.optimization_barrier(block_part.astype(jnp.bfloat16)).astype(jnp.float32)
                return (running + block_part, None)
            running, _ = lax.scan(add_angle, jnp.zeros((BLOCKS, TILE, SLICES), jnp.float32), angles)
            return running
        gradient = lax.map(backproject, spaces).reshape(N_SPACE * BLOCKS * TILE, SLICES)
        current = jnp.maximum(current - step_size * gradient, 0.0)
    return (current, residual)
```

```python
import functools
import math

import jax
import jax.numpy as jnp
from jax import lax
from jax.experimental import pallas as pl
from jax.experimental.pallas import tpu as pltpu
from jax.sharding import PartitionSpec as P

CAP = 2
ITERS = 2
MESH = pl.DeviceIdType.MESH
F32 = jnp.float32
BF16 = jnp.bfloat16


def kernel(
    dims, image, tiles, slot_row, block_row, ray_list, sinogram, weights, volume, residual,
    tile_v, run_f, run_t, mat, mat_t, pix, acc, part, ray_in, ray_res, ray_out, slot_res,
    grad_out, grad_in, chain_out, chain_dn, chain_up, key_v, table_v, table_s, ids_out, ids_in,
    ids_s, local_sem, ag_send, ag_recv, id_send, id_recv, ray_send, ray_recv, back_send,
    back_recv, gx_send, gx_recv, dn_send, dn_recv, up_send, up_recv,
):
    n_space, n_angle, nx, nz, edge, own, slots, step_size = dims
    count = tiles.shape[0]
    width = key_v.shape[1]
    share = image.shape[0]
    per_chunk = share // edge
    blocks = per_chunk * n_angle
    seats = n_space * CAP
    me_s = lax.axis_index("space")
    me_a = lax.axis_index("angle")
    z, x = me_a // nx, me_a % nx
    has_up, has_dn = z < nz - 1, z > 0
    x_peers = [(x + j) % nx for j in range(1, nx)]
    s_peers = [(me_s + j) % n_space for j in range(1, n_space)]

    def at_angle(zz, xx):
        return (me_s, zz * nx + xx)

    def remote(src, dst, send, recv, device):
        return pltpu.make_async_remote_copy(
            src_ref=src, dst_ref=dst, send_sem=send, recv_sem=recv, device_id=device,
            device_id_type=MESH,
        )

    barrier = pltpu.get_barrier_semaphore()

    def greet(device):
        pl.semaphore_signal(barrier, inc=1, device_id=device, device_id_type=MESH)

    @pl.when(has_up)
    def _():
        greet(at_angle(z + 1, x))

    @pl.when(has_dn)
    def _():
        greet(at_angle(z - 1, x))

    for xx in x_peers:
        greet(at_angle(z, xx))
    for ss in s_peers:
        greet((ss, me_a))
    tile_copy = pltpu.make_async_copy(tiles, tile_v.at[pl.ds(0, count)], local_sem.at[0])
    tile_copy.start()
    volume[...] = image[...]
    pix[me_a] = image[...].astype(BF16)
    friends = has_up.astype(jnp.int32) + has_dn.astype(jnp.int32) + (nx - 1 + n_space - 1)
    pl.semaphore_wait(barrier, friends)

    def ag_copy(kind, src_a, device):
        return remote(
            pix.at[src_a], pix.at[src_a], ag_send.at[kind, src_a], ag_recv.at[src_a], device
        )

    def ag_copies(src_z, go_up, go_dn):
        src_a = src_z * nx + x
        listed = []
        if go_up:
            listed.append((has_up, ag_copy(0, src_a, at_angle(jnp.minimum(z + 1, nz - 1), x))))
        if go_dn:
            listed.append((has_dn, ag_copy(1, src_a, at_angle(jnp.maximum(z - 1, 0), x))))
        for j, xx in enumerate(x_peers):
            listed.append((None, ag_copy(2 + j, src_a, at_angle(z, xx))))
        return listed

    def each(listed, act):
        for cond, copy in listed:
            if cond is None:
                act(copy)
            else:
                pl.when(cond)(functools.partial(act, copy))

    def start(copy):
        copy.start()

    def wait_send(copy):
        copy.wait_send()

    def ag_wait(src_a):
        ag_copy(0, src_a, (me_s, me_a)).wait_recv()

    def gather(work):
        each(ag_copies(z, True, True), start)
        work(0)
        for k in range(1, nz):

            @pl.when(z - k >= 0)
            def _():
                ag_wait((z - k) * nx + x)
                each(ag_copies(z - k, True, False), start)

            @pl.when(z + k < nz)
            def _():
                ag_wait((z + k) * nx + x)
                each(ag_copies(z + k, False, True), start)

            work(k)

    def gather_end():
        each(ag_copies(z, True, True), wait_send)
        for k in range(1, nz):

            @pl.when(z - k >= 0)
            def _():
                each(ag_copies(z - k, True, False), wait_send)

            @pl.when(z + k < nz)
            def _():
                each(ag_copies(z + k, False, True), wait_send)

    def prepare():
        rays = [ray_list[0, j] for j in range(slots)]
        owners = [r // own for r in rays]
        seat = []
        for j in range(slots):
            rank = jnp.int32(0)
            for i in range(j):
                rank = rank + (owners[i] == owners[j]).astype(jnp.int32)
            seat.append(owners[j] * CAP + rank)
        for p in range(seats):
            local = jnp.int32(-1)
            for j in range(slots):
                local = jnp.where(seat[j] == p, rays[j] % own, local)
            ids_out[p // CAP, p % CAP, :] = jnp.full((128,), local, jnp.int32)
        ids_in[me_s] = ids_out[me_s]
        for j, ss in enumerate(s_peers):
            remote(
                ids_out.at[ss], ids_in.at[me_s], id_send.at[j], id_recv.at[me_s], (ss, me_a)
            ).start()
        spread = jnp.zeros((1, count), jnp.int32)
        for j in range(slots):
            spread = jnp.where(slot_row[...] == j, seat[j], spread)
        key_v[...] = jnp.full(key_v.shape, -1, jnp.int32)
        key_v[0:1, 0:count] = spread * blocks + block_row[...]
        across = jnp.broadcast_to(key_v[0:1, :], (width, width))
        down = across.T
        u = lax.broadcasted_iota(jnp.int32, (width, width), 0)
        t = lax.broadcasted_iota(jnp.int32, (width, width), 1)
        before = jnp.max(jnp.where((across == down) & (u < t), u, -1), axis=0, keepdims=True)
        table_v[0:1, :] = jnp.where(before < 0, count, before)
        for j in range(-(-seats * blocks // width)):
            last = jnp.max(jnp.where(down == t + j * width, u, -1), axis=0, keepdims=True)
            table_v[1 + j : 2 + j, :] = jnp.where(last < 0, count, last)
        copy = pltpu.make_async_copy(table_v, table_s, local_sem.at[1])
        copy.start()
        copy.wait()
        run_f[count] = jnp.zeros((edge, edge), F32)
        run_t[count] = jnp.zeros((edge, edge), BF16)
        tile_copy.wait()
        tile_v[count] = jnp.zeros((edge, edge), BF16)

    def run_tiles(begin, end):
        @pl.loop(begin, end)
        def _(t):
            total = tile_v[t].astype(F32) + run_f[table_s[0, t]]
            run_f[t] = total
            tile_v[t] = total.astype(BF16)
            run_t[t] = total.T.astype(BF16)

    def build(begin, end):
        @pl.loop(begin, end)
        def _(c):
            for p in range(seats):
                for q in range(per_chunk):
                    cell = p * blocks + c * per_chunk + q
                    which = table_s[1 + cell // width, cell % width]
                    mat[c, p * edge : (p + 1) * edge, q * edge : (q + 1) * edge] = tile_v[which]
                    mat_t[c, q * edge : (q + 1) * edge, p * edge : (p + 1) * edge] = run_t[which]

    def project(c):
        acc[0 : seats * edge] += jnp.dot(mat[c], pix[c], preferred_element_type=F32)

    def first_work(k):
        half = count // 2
        if k == 0:
            prepare()
            run_tiles(0, half)
        if k == min(1, nz - 1):
            run_tiles(half, count)
        if k == min(2, nz - 1):
            build(0, n_angle)

    def across_x(src_z):
        for xx in x_peers:
            ag_wait(src_z * nx + xx)
            project(src_z * nx + xx)

    def later_work(k):
        if k == 0:
            acc[...] = jnp.zeros(acc.shape, F32)
            project(me_a)
            return

        @pl.when(z - k >= 0)
        def _():
            project((z - k) * nx + x)

        @pl.when(z + k < nz)
        def _():
            project((z + k) * nx + x)

        if k == 1:
            across_x(z)
        else:

            @pl.when(z - k + 1 >= 0)
            def _():
                across_x(z - k + 1)

            @pl.when(z + k - 1 < nz)
            def _():
                across_x(z + k - 1)

    def later_end():
        k = nz - 1

        @pl.when(z - k >= 0)
        def _():
            across_x(z - k)

        @pl.when(z + k < nz)
        def _():
            across_x(z + k)

    def first_end():
        acc[...] = jnp.zeros(acc.shape, F32)
        for zz in range(nz):
            for xx in x_peers:
                ag_wait(zz * nx + xx)

        @pl.loop(0, n_angle)
        def _(c):
            project(c)

    group = CAP * edge

    def ray_copy(j, ss):
        return remote(
            part.at[pl.ds(ss * CAP, CAP)], ray_in.at[pl.ds(me_s * CAP, CAP)],
            ray_send.at[j], ray_recv.at[me_s], (ss, me_a),
        )

    def ray_wait(ss):
        rows = pl.ds(ss * CAP, CAP)
        remote(
            part.at[rows], ray_in.at[rows], ray_send.at[0], ray_recv.at[ss], (ss, me_a)
        ).wait_recv()

    def back_copy(j, ss):
        return remote(
            ray_out.at[pl.ds(ss * group, group)], slot_res.at[pl.ds(me_s * group, group)],
            back_send.at[j], back_recv.at[me_s], (ss, me_a),
        )

    def back_wait(ss):
        rows = pl.ds(ss * group, group)
        remote(
            ray_out.at[rows], slot_res.at[rows], back_send.at[0], back_recv.at[ss], (ss, me_a)
        ).wait_recv()

    def exchange(first):
        part[...] = acc[0 : seats * edge].astype(BF16).reshape(part.shape)
        for j, ss in enumerate(s_peers):
            ray_copy(j, ss).start()
        mine = pl.ds(me_s * CAP, CAP)
        ray_in[mine] = part[mine]
        if first:
            ray_in[seats] = jnp.zeros((edge, edge), BF16)
            ray_res[own] = jnp.zeros((edge, edge), BF16)
            for j, ss in enumerate(s_peers):
                copy = remote(
                    ids_out.at[ss], ids_in.at[ss], id_send.at[j], id_recv.at[ss], (ss, me_a)
                )
                copy.wait_send()
                copy.wait_recv()
            copy = pltpu.make_async_copy(ids_in, ids_s, local_sem.at[1])
            copy.start()
            copy.wait()
        for ss in s_peers:
            ray_wait(ss)
        for o in range(own):
            total = -sinogram[o].astype(F32)
            for ss in range(n_space):
                where = jnp.int32(seats)
                for c in range(CAP):
                    where = jnp.where(ids_s[ss, c, 0] == o, ss * CAP + c, where)
                total = total + ray_in[where].astype(F32)
            ray_res[o] = (weights[o].astype(F32) * total).astype(BF16)
        for j, ss in enumerate(s_peers):
            for c in range(CAP):
                which = ids_s[ss, c, 0]
                which = jnp.where(which < 0, own, which)
                ray_out[pl.ds(ss * group + c * edge, edge)] = ray_res[which]
            back_copy(j, ss).start()
        for c in range(CAP):
            which = ids_s[me_s, c, 0]
            which = jnp.where(which < 0, own, which)
            slot_res[pl.ds(me_s * group + c * edge, edge)] = ray_res[which]
        for ss in s_peers:
            back_wait(ss)

    def exchange_end():
        for j, ss in enumerate(s_peers):
            ray_copy(j, ss).wait_send()
            back_copy(j, ss).wait_send()

    def gx_copy(dst_z, j, xx):
        return remote(
            grad_out.at[dst_z, j], grad_in.at[dst_z, j], gx_send.at[dst_z, j],
            gx_recv.at[dst_z, j], at_angle(z, xx),
        )

    def dn_copy(dst_z):
        return remote(
            chain_out.at[dst_z], chain_dn.at[dst_z], dn_send.at[dst_z], dn_recv.at[dst_z],
            at_angle(jnp.maximum(z - 1, 0), x),
        )

    def up_copy(dst_z):
        return remote(
            chain_out.at[dst_z], chain_up.at[dst_z], up_send.at[dst_z], up_recv.at[dst_z],
            at_angle(jnp.minimum(z + 1, nz - 1), x),
        )

    def back(c):
        return jnp.dot(mat_t[c], slot_res[...], preferred_element_type=F32)

    def send_terms(dst_z):
        for j, xx in enumerate(x_peers):
            grad_out[dst_z, j] = back(dst_z * nx + xx).astype(BF16)
            gx_copy(dst_z, j, xx).start()

    def sum_terms(dst_z):
        acc[0:share] = back(dst_z * nx + x)
        for j in range(nx - 1):
            gx_copy(dst_z, j, x_peers[j]).wait_recv()
            acc[0:share] += grad_in[dst_z, j].astype(F32)

    def add_dn(dst_z):
        dn_copy(dst_z).wait_recv()
        acc[0:share] += chain_dn[dst_z].astype(F32)

    def add_up(dst_z):
        up_copy(dst_z).wait_recv()
        acc[0:share] += chain_up[dst_z].astype(F32)

    def scatter():
        for k in range(nz - 1, 0, -1):

            @pl.when(z - k >= 0)
            def _():
                send_terms(z - k)

            @pl.when(z + k < nz)
            def _():
                send_terms(z + k)

        send_terms(z)
        for k in range(nz - 1, 0, -1):

            @pl.when(z - k >= 0)
            def _():
                sum_terms(z - k)
                pl.when(has_up)(functools.partial(add_dn, z - k))
                chain_out[z - k] = acc[0:share].astype(BF16)
                dn_copy(z - k).start()

            @pl.when(z + k < nz)
            def _():
                sum_terms(z + k)
                pl.when(has_dn)(functools.partial(add_up, z + k))
                chain_out[z + k] = acc[0:share].astype(BF16)
                up_copy(z + k).start()

        sum_terms(z)
        pl.when(has_up)(functools.partial(add_dn, z))
        pl.when(has_dn)(functools.partial(add_up, z))
        volume[...] = jnp.maximum(volume[...] - step_size * acc[0:share], 0.0)

    def scatter_end():
        for dst_z in range(nz):
            for j, xx in enumerate(x_peers):
                gx_copy(dst_z, j, xx).wait_send()

            @pl.when(z > dst_z)
            def _():
                dn_copy(dst_z).wait_send()

            @pl.when(z < dst_z)
            def _():
                up_copy(dst_z).wait_send()

    for iteration in range(ITERS):
        if iteration == 0:
            gather(first_work)
            first_end()
        else:
            pix[me_a] = volume[...].astype(BF16)
            gather(later_work)
            later_end()
        exchange(iteration == 0)
        gather_end()
        scatter()
        exchange_end()
        scatter_end()
    residual[...] = ray_res[0:own]


def shards(image, tiles, tile_slot, tile_block, slot_ray, sinogram, weights):
    n_space = lax.axis_size("space")
    n_angle = lax.axis_size("angle")
    tile_mats = tiles[0]
    count, edge = tile_mats.shape[:2]
    slices = image.shape[1]
    share = image.shape[0]
    own = sinogram.shape[1]
    slots = slot_ray.shape[1]
    blocks = share * n_angle // edge
    seats = n_space * CAP
    nx = max(1, math.isqrt(n_angle // 2))
    while n_angle % nx:
        nx -= 1
    nz = n_angle // nx
    width = -(-count // 128) * 128
    table = -(-(1 + -(-seats * blocks // width)) // 8) * 8
    step_size = 0.2 * math.sqrt(blocks / (n_angle * own))
    dims = (n_space, n_angle, nx, nz, edge, own, slots, step_size)
    vmem, dma = pltpu.VMEM, pltpu.SemaphoreType.DMA
    others, sides = n_space - 1, nx - 1
    whole = pl.BlockSpec(memory_space=pltpu.VMEM)
    volume, residual = pl.pallas_call(
        functools.partial(kernel, dims),
        out_shape=(
            jax.ShapeDtypeStruct((share, slices), F32),
            jax.ShapeDtypeStruct((own, edge, slices), BF16),
        ),
        in_specs=[
            whole, pl.BlockSpec(memory_space=pl.ANY), whole, whole,
            pl.BlockSpec(memory_space=pltpu.SMEM), whole, whole,
        ],
        out_specs=(whole, whole),
        scratch_shapes=[
            vmem((count + 1, edge, edge), BF16),
            vmem((count + 1, edge, edge), F32),
            vmem((count + 1, edge, edge), BF16),
            vmem((n_angle, seats * edge, share), BF16),
            vmem((n_angle, share, seats * edge), BF16),
            vmem((n_angle, share, slices), BF16),
            vmem((max(seats * edge, share), slices), F32),
            vmem((seats, edge, slices), BF16),
            vmem((seats + 1, edge, slices), BF16),
            vmem((own + 1, edge, slices), BF16),
            vmem((seats * edge, slices), BF16),
            vmem((seats * edge, slices), BF16),
            vmem((nz, sides, share, slices), BF16),
            vmem((nz, sides, share, slices), BF16),
            vmem((nz, share, slices), BF16),
            vmem((nz, share, slices), BF16),
            vmem((nz, share, slices), BF16),
            vmem((8, width), jnp.int32),
            vmem((table, width), jnp.int32),
            pltpu.SMEM((table, width), jnp.int32),
            vmem((n_space, 8, 128), jnp.int32),
            vmem((n_space, 8, 128), jnp.int32),
            pltpu.SMEM((n_space, 8, 128), jnp.int32),
            dma((2,)),
            dma((2 + sides, n_angle)), dma((n_angle,)),
            dma((others,)), dma((n_space,)),
            dma((others,)), dma((n_space,)),
            dma((others,)), dma((n_space,)),
            dma((nz, sides)), dma((nz, sides)),
            dma((nz,)), dma((nz,)),
            dma((nz,)), dma((nz,)),
        ],
        compiler_params=pltpu.CompilerParams(
            collective_id=0, has_side_effects=True, vmem_limit_bytes=58 * 1024 * 1024
        ),
    )(image, tile_mats, tile_slot, tile_block, slot_ray, sinogram[0], weights[0])
    return (volume, residual[None])


def solution(mesh):
    placed = (
        P(("space", "angle"), None),
        P("space", "angle", None, None),
        P("space", "angle"),
        P("space", "angle"),
        P("space", "angle"),
        P("angle", "space", None, None),
        P("angle", "space", None, None),
    )
    return jax.shard_map(
        shards,
        mesh=mesh,
        in_specs=placed,
        out_specs=(P(("space", "angle"), None), P("angle", "space", None, None)),
        check_vma=False,
    )
```

```python
import functools
import math

import jax
import jax.numpy as jnp
from jax import lax
from jax.experimental import pallas as pl
from jax.experimental.pallas import tpu as pltpu
from jax.sharding import PartitionSpec as P

CAP = 2
ITERS = 2
PARTS = 2
MESH = pl.DeviceIdType.MESH
F32 = jnp.float32
BF16 = jnp.bfloat16


def kernel(
    dims, image, tiles, slot_row, block_row, ray_list, sinogram, weights, volume, residual,
    tile_v, run_f, run_t, mat, mat_t, pix, acc, part, ray_in, ray_res, ray_out, slot_res,
    grad_out, grad_in, chain_out, chain_dn, chain_up, key_v, table_v, table_s, ids_out, ids_in,
    ids_s, local_sem, ag_send, ag_recv, id_send, id_recv, ray_send, ray_recv, back_send,
    back_recv, gx_send, gx_recv, dn_send, dn_recv, up_send, up_recv,
):
    n_space, n_angle, nx, nz, edge, own, slots, step_size = dims
    count = tiles.shape[0]
    width = key_v.shape[1]
    share = image.shape[0]
    per_chunk = share // edge
    blocks = per_chunk * n_angle
    seats = n_space * CAP
    me_s = lax.axis_index("space")
    me_a = lax.axis_index("angle")
    z, x = me_a // nx, me_a % nx
    has_up, has_dn = z < nz - 1, z > 0
    x_peers = [(x + j) % nx for j in range(1, nx)]
    s_peers = [(me_s + j) % n_space for j in range(1, n_space)]

    def at_angle(zz, xx):
        return (me_s, zz * nx + xx)

    def remote(src, dst, send, recv, device):
        return pltpu.make_async_remote_copy(
            src_ref=src, dst_ref=dst, send_sem=send, recv_sem=recv, device_id=device,
            device_id_type=MESH,
        )

    barrier = pltpu.get_barrier_semaphore()

    def greet(device):
        pl.semaphore_signal(barrier, inc=1, device_id=device, device_id_type=MESH)

    @pl.when(has_up)
    def _():
        greet(at_angle(z + 1, x))

    @pl.when(has_dn)
    def _():
        greet(at_angle(z - 1, x))

    for xx in x_peers:
        greet(at_angle(z, xx))
    for ss in s_peers:
        greet((ss, me_a))
    tile_copy = pltpu.make_async_copy(tiles, tile_v.at[pl.ds(0, count)], local_sem.at[0])
    tile_copy.start()
    volume[...] = image[...]
    pix[me_a] = image[...].astype(BF16)
    friends = has_up.astype(jnp.int32) + has_dn.astype(jnp.int32) + (nx - 1 + n_space - 1)
    pl.semaphore_wait(barrier, friends)

    piece = share // PARTS

    def rows_of(h):
        return pl.ds(h * piece, piece)

    def ag_copy(kind, src_a, h, device):
        rows = pix.at[src_a, rows_of(h)]
        return remote(rows, rows, ag_send.at[kind, src_a, h], ag_recv.at[src_a, h], device)

    def ag_copies(src_z, h, go_up, go_dn):
        src_a = src_z * nx + x
        listed = []
        if go_up:
            listed.append((has_up, ag_copy(0, src_a, h, at_angle(jnp.minimum(z + 1, nz - 1), x))))
        if go_dn:
            listed.append((has_dn, ag_copy(1, src_a, h, at_angle(jnp.maximum(z - 1, 0), x))))
        for j, xx in enumerate(x_peers):
            listed.append((None, ag_copy(2 + j, src_a, h, at_angle(z, xx))))
        return listed

    def each(listed, act):
        for cond, copy in listed:
            if cond is None:
                act(copy)
            else:
                pl.when(cond)(functools.partial(act, copy))

    def start(copy):
        copy.start()

    def wait_send(copy):
        copy.wait_send()

    def ag_wait(src_a, h):
        ag_copy(0, src_a, h, (me_s, me_a)).wait_recv()

    def gather(work):
        for h in range(PARTS):
            each(ag_copies(z, h, True, True), start)
        work(0, PARTS - 1)
        for k in range(1, nz):
            for h in range(PARTS):

                @pl.when(z - k >= 0)
                def _():
                    ag_wait((z - k) * nx + x, h)
                    each(ag_copies(z - k, h, True, False), start)

                @pl.when(z + k < nz)
                def _():
                    ag_wait((z + k) * nx + x, h)
                    each(ag_copies(z + k, h, False, True), start)

                work(k, h)

    def gather_end():
        for h in range(PARTS):
            each(ag_copies(z, h, True, True), wait_send)
            for k in range(1, nz):

                @pl.when(z - k >= 0)
                def _():
                    each(ag_copies(z - k, h, True, False), wait_send)

                @pl.when(z + k < nz)
                def _():
                    each(ag_copies(z + k, h, False, True), wait_send)

    def prepare():
        rays = [ray_list[0, j] for j in range(slots)]
        owners = [r // own for r in rays]
        seat = []
        for j in range(slots):
            rank = jnp.int32(0)
            for i in range(j):
                rank = rank + (owners[i] == owners[j]).astype(jnp.int32)
            seat.append(owners[j] * CAP + rank)
        for p in range(seats):
            local = jnp.int32(-1)
            for j in range(slots):
                local = jnp.where(seat[j] == p, rays[j] % own, local)
            ids_out[p // CAP, p % CAP, :] = jnp.full((128,), local, jnp.int32)
        ids_in[me_s] = ids_out[me_s]
        for j, ss in enumerate(s_peers):
            remote(
                ids_out.at[ss], ids_in.at[me_s], id_send.at[j], id_recv.at[me_s], (ss, me_a)
            ).start()
        spread = jnp.zeros((1, count), jnp.int32)
        for j in range(slots):
            spread = jnp.where(slot_row[...] == j, seat[j], spread)
        key_v[...] = jnp.full(key_v.shape, -1, jnp.int32)
        key_v[0:1, 0:count] = spread * blocks + block_row[...]
        across = jnp.broadcast_to(key_v[0:1, :], (width, width))
        down = across.T
        u = lax.broadcasted_iota(jnp.int32, (width, width), 0)
        t = lax.broadcasted_iota(jnp.int32, (width, width), 1)
        before = jnp.max(jnp.where((across == down) & (u < t), u, -1), axis=0, keepdims=True)
        table_v[0:1, :] = jnp.where(before < 0, count, before)
        for j in range(-(-seats * blocks // width)):
            last = jnp.max(jnp.where(down == t + j * width, u, -1), axis=0, keepdims=True)
            table_v[1 + j : 2 + j, :] = jnp.where(last < 0, count, last)
        copy = pltpu.make_async_copy(table_v, table_s, local_sem.at[1])
        copy.start()
        copy.wait()
        run_f[count] = jnp.zeros((edge, edge), F32)
        run_t[count] = jnp.zeros((edge, edge), BF16)
        tile_copy.wait()
        tile_v[count] = jnp.zeros((edge, edge), BF16)

    def run_tiles(begin, end):
        @pl.loop(begin, end)
        def _(t):
            total = tile_v[t].astype(F32) + run_f[table_s[0, t]]
            run_f[t] = total
            tile_v[t] = total.astype(BF16)
            run_t[t] = total.T.astype(BF16)

    def build(begin, end):
        @pl.loop(begin, end)
        def _(c):
            for p in range(seats):
                for q in range(per_chunk):
                    cell = p * blocks + c * per_chunk + q
                    which = table_s[1 + cell // width, cell % width]
                    mat[c, p * edge : (p + 1) * edge, q * edge : (q + 1) * edge] = tile_v[which]
                    mat_t[c, q * edge : (q + 1) * edge, p * edge : (p + 1) * edge] = run_t[which]

    def project(c):
        acc[0 : seats * edge] += jnp.dot(mat[c], pix[c], preferred_element_type=F32)

    def first_work(k, h):
        slot = max(k - 1, 0) * PARTS + h
        splits = max((nz - 1) * PARTS, 1)
        turns = max(splits - PARTS, 1)
        if k == 0:
            prepare()
        if k == 0 and nz > 1:
            return
        if slot < turns:
            run_tiles(count * slot // turns, count * (slot + 1) // turns)
        if slot == splits - 1:
            build(0, n_angle)

    def across_x(src_z):
        for xx in x_peers:
            for h in range(PARTS):
                ag_wait(src_z * nx + xx, h)
            project(src_z * nx + xx)

    def later_work(k, h):
        if k == 0:
            acc[...] = jnp.zeros(acc.shape, F32)
            project(me_a)
            return
        if h < PARTS - 1:
            if k == 1:
                across_x(z)
                return

            @pl.when(z - k + 1 >= 0)
            def _():
                across_x(z - k + 1)

            @pl.when(z + k - 1 < nz)
            def _():
                across_x(z + k - 1)

            return

        @pl.when(z - k >= 0)
        def _():
            project((z - k) * nx + x)

        @pl.when(z + k < nz)
        def _():
            project((z + k) * nx + x)

    def later_end():
        k = nz - 1

        @pl.when(z - k >= 0)
        def _():
            across_x(z - k)

        @pl.when(z + k < nz)
        def _():
            across_x(z + k)

    def first_end():
        acc[...] = jnp.zeros(acc.shape, F32)
        for zz in range(nz):
            for xx in x_peers:
                for h in range(PARTS):
                    ag_wait(zz * nx + xx, h)

        @pl.loop(0, n_angle)
        def _(c):
            project(c)

    group = CAP * edge

    def ray_copy(j, ss):
        return remote(
            part.at[pl.ds(ss * CAP, CAP)], ray_in.at[pl.ds(me_s * CAP, CAP)],
            ray_send.at[j], ray_recv.at[me_s], (ss, me_a),
        )

    def ray_wait(ss):
        rows = pl.ds(ss * CAP, CAP)
        remote(
            part.at[rows], ray_in.at[rows], ray_send.at[0], ray_recv.at[ss], (ss, me_a)
        ).wait_recv()

    def back_copy(j, ss):
        return remote(
            ray_out.at[pl.ds(ss * group, group)], slot_res.at[pl.ds(me_s * group, group)],
            back_send.at[j], back_recv.at[me_s], (ss, me_a),
        )

    def back_wait(ss):
        rows = pl.ds(ss * group, group)
        remote(
            ray_out.at[rows], slot_res.at[rows], back_send.at[0], back_recv.at[ss], (ss, me_a)
        ).wait_recv()

    def exchange(first):
        part[...] = acc[0 : seats * edge].astype(BF16).reshape(part.shape)
        for j, ss in enumerate(s_peers):
            ray_copy(j, ss).start()
        mine = pl.ds(me_s * CAP, CAP)
        ray_in[mine] = part[mine]
        if first:
            ray_in[seats] = jnp.zeros((edge, edge), BF16)
            ray_res[own] = jnp.zeros((edge, edge), BF16)
            for j, ss in enumerate(s_peers):
                copy = remote(
                    ids_out.at[ss], ids_in.at[ss], id_send.at[j], id_recv.at[ss], (ss, me_a)
                )
                copy.wait_send()
                copy.wait_recv()
            copy = pltpu.make_async_copy(ids_in, ids_s, local_sem.at[1])
            copy.start()
            copy.wait()
        for ss in s_peers:
            ray_wait(ss)
        for o in range(own):
            total = -sinogram[o].astype(F32)
            for ss in range(n_space):
                where = jnp.int32(seats)
                for c in range(CAP):
                    where = jnp.where(ids_s[ss, c, 0] == o, ss * CAP + c, where)
                total = total + ray_in[where].astype(F32)
            ray_res[o] = (weights[o].astype(F32) * total).astype(BF16)
        for j, ss in enumerate(s_peers):
            for c in range(CAP):
                which = ids_s[ss, c, 0]
                which = jnp.where(which < 0, own, which)
                ray_out[pl.ds(ss * group + c * edge, edge)] = ray_res[which]
            back_copy(j, ss).start()
        for c in range(CAP):
            which = ids_s[me_s, c, 0]
            which = jnp.where(which < 0, own, which)
            slot_res[pl.ds(me_s * group + c * edge, edge)] = ray_res[which]
        for ss in s_peers:
            back_wait(ss)

    def exchange_end():
        for j, ss in enumerate(s_peers):
            ray_copy(j, ss).wait_send()
            back_copy(j, ss).wait_send()

    def gx_copy(dst_z, j, h, xx):
        rows = (dst_z, j, rows_of(h))
        sem = (dst_z, j, h)
        return remote(
            grad_out.at[rows], grad_in.at[rows], gx_send.at[sem], gx_recv.at[sem], at_angle(z, xx)
        )

    def dn_copy(dst_z, h):
        rows = (dst_z, rows_of(h))
        return remote(
            chain_out.at[rows], chain_dn.at[rows], dn_send.at[dst_z, h], dn_recv.at[dst_z, h],
            at_angle(jnp.maximum(z - 1, 0), x),
        )

    def up_copy(dst_z, h):
        rows = (dst_z, rows_of(h))
        return remote(
            chain_out.at[rows], chain_up.at[rows], up_send.at[dst_z, h], up_recv.at[dst_z, h],
            at_angle(jnp.minimum(z + 1, nz - 1), x),
        )

    def back(c, h):
        return jnp.dot(mat_t[c, rows_of(h)], slot_res[...], preferred_element_type=F32)

    def send_terms(dst_z, h):
        for j, xx in enumerate(x_peers):
            grad_out[dst_z, j, rows_of(h)] = back(dst_z * nx + xx, h).astype(BF16)
            gx_copy(dst_z, j, h, xx).start()

    def sum_terms(dst_z, h):
        total = back(dst_z * nx + x, h)
        for j in range(nx - 1):
            gx_copy(dst_z, j, h, x_peers[j]).wait_recv()
            total = total + grad_in[dst_z, j, rows_of(h)].astype(F32)
        acc[0:piece] = total

    def add_dn(dst_z, h):
        dn_copy(dst_z, h).wait_recv()
        acc[0:piece] += chain_dn[dst_z, rows_of(h)].astype(F32)

    def add_up(dst_z, h):
        up_copy(dst_z, h).wait_recv()
        acc[0:piece] += chain_up[dst_z, rows_of(h)].astype(F32)

    def scatter():
        for k in range(nz - 1, 0, -1):
            for h in range(PARTS):

                @pl.when(z - k >= 0)
                def _():
                    send_terms(z - k, h)

                @pl.when(z + k < nz)
                def _():
                    send_terms(z + k, h)

        for h in range(PARTS):
            send_terms(z, h)
        for k in range(nz - 1, 0, -1):
            for h in range(PARTS):

                @pl.when(z - k >= 0)
                def _():
                    sum_terms(z - k, h)
                    pl.when(has_up)(functools.partial(add_dn, z - k, h))
                    chain_out[z - k, rows_of(h)] = acc[0:piece].astype(BF16)
                    dn_copy(z - k, h).start()

                @pl.when(z + k < nz)
                def _():
                    sum_terms(z + k, h)
                    pl.when(has_dn)(functools.partial(add_up, z + k, h))
                    chain_out[z + k, rows_of(h)] = acc[0:piece].astype(BF16)
                    up_copy(z + k, h).start()

        for h in range(PARTS):
            sum_terms(z, h)
            pl.when(has_up)(functools.partial(add_dn, z, h))
            pl.when(has_dn)(functools.partial(add_up, z, h))
            rows = rows_of(h)
            volume[rows] = jnp.maximum(volume[rows] - step_size * acc[0:piece], 0.0)

    def scatter_end():
        for dst_z in range(nz):
            for h in range(PARTS):
                for j, xx in enumerate(x_peers):
                    gx_copy(dst_z, j, h, xx).wait_send()

                @pl.when(z > dst_z)
                def _():
                    dn_copy(dst_z, h).wait_send()

                @pl.when(z < dst_z)
                def _():
                    up_copy(dst_z, h).wait_send()

    for iteration in range(ITERS):
        if iteration == 0:
            gather(first_work)
            first_end()
        else:
            pix[me_a] = volume[...].astype(BF16)
            gather(later_work)
            later_end()
        exchange(iteration == 0)
        gather_end()
        scatter()
        exchange_end()
        scatter_end()
    residual[...] = ray_res[0:own]


def hand_out(volume, residual, volume_out, residual_out):
    volume_out[...] = volume[...]
    residual_out[...] = residual[...]


def shards(image, tiles, tile_slot, tile_block, slot_ray, sinogram, weights):
    n_space = lax.axis_size("space")
    n_angle = lax.axis_size("angle")
    tile_mats = tiles[0]
    count, edge = tile_mats.shape[:2]
    slices = image.shape[1]
    share = image.shape[0]
    own = sinogram.shape[1]
    slots = slot_ray.shape[1]
    blocks = share * n_angle // edge
    seats = n_space * CAP
    nx = max(1, math.isqrt(n_angle // 2))
    while n_angle % nx:
        nx -= 1
    nz = n_angle // nx
    width = -(-count // 128) * 128
    table = -(-(1 + -(-seats * blocks // width)) // 8) * 8
    step_size = 0.2 * math.sqrt(blocks / (n_angle * own))
    dims = (n_space, n_angle, nx, nz, edge, own, slots, step_size)
    vmem, dma = pltpu.VMEM, pltpu.SemaphoreType.DMA
    others, sides = n_space - 1, nx - 1
    whole = pl.BlockSpec(memory_space=pltpu.VMEM)
    volume, residual = pl.pallas_call(
        functools.partial(kernel, dims),
        out_shape=(
            jax.ShapeDtypeStruct((share, slices), F32),
            jax.ShapeDtypeStruct((own, edge, slices), BF16),
        ),
        in_specs=[
            whole, pl.BlockSpec(memory_space=pl.ANY), whole, whole,
            pl.BlockSpec(memory_space=pltpu.SMEM), whole, whole,
        ],
        out_specs=(whole, whole),
        scratch_shapes=[
            vmem((count + 1, edge, edge), BF16),
            vmem((count + 1, edge, edge), F32),
            vmem((count + 1, edge, edge), BF16),
            vmem((n_angle, seats * edge, share), BF16),
            vmem((n_angle, share, seats * edge), BF16),
            vmem((n_angle, share, slices), BF16),
            vmem((max(seats * edge, share), slices), F32),
            vmem((seats, edge, slices), BF16),
            vmem((seats + 1, edge, slices), BF16),
            vmem((own + 1, edge, slices), BF16),
            vmem((seats * edge, slices), BF16),
            vmem((seats * edge, slices), BF16),
            vmem((nz, sides, share, slices), BF16),
            vmem((nz, sides, share, slices), BF16),
            vmem((nz, share, slices), BF16),
            vmem((nz, share, slices), BF16),
            vmem((nz, share, slices), BF16),
            vmem((8, width), jnp.int32),
            vmem((table, width), jnp.int32),
            pltpu.SMEM((table, width), jnp.int32),
            vmem((n_space, 8, 128), jnp.int32),
            vmem((n_space, 8, 128), jnp.int32),
            pltpu.SMEM((n_space, 8, 128), jnp.int32),
            dma((2,)),
            dma((2 + sides, n_angle, PARTS)), dma((n_angle, PARTS)),
            dma((others,)), dma((n_space,)),
            dma((others,)), dma((n_space,)),
            dma((others,)), dma((n_space,)),
            dma((nz, sides, PARTS)), dma((nz, sides, PARTS)),
            dma((nz, PARTS)), dma((nz, PARTS)),
            dma((nz, PARTS)), dma((nz, PARTS)),
        ],
        compiler_params=pltpu.CompilerParams(
            collective_id=0, has_side_effects=True, vmem_limit_bytes=58 * 1024 * 1024
        ),
    )(image, tile_mats, tile_slot, tile_block, slot_ray, sinogram[0], weights[0])
    volume, residual = pl.pallas_call(
        hand_out,
        out_shape=(
            jax.ShapeDtypeStruct(volume.shape, F32),
            jax.ShapeDtypeStruct(residual.shape, BF16),
        ),
        in_specs=[whole, whole],
        out_specs=(whole, whole),
    )(volume, residual)
    return (volume, residual[None])


def solution(mesh):
    placed = (
        P(("space", "angle"), None),
        P("space", "angle", None, None),
        P("space", "angle"),
        P("space", "angle"),
        P("space", "angle"),
        P("angle", "space", None, None),
        P("angle", "space", None, None),
    )
    return jax.shard_map(
        shards,
        mesh=mesh,
        in_specs=placed,
        out_specs=(P(("space", "angle"), None), P("angle", "space", None, None)),
        check_vma=False,
    )
```

```python
import functools
import math

import jax
import jax.numpy as jnp
from jax import lax
from jax.experimental import pallas as pl
from jax.experimental.pallas import tpu as pltpu
from jax.sharding import PartitionSpec as P

CAP = 2
ITERS = 2
PARTS = 4
MESH = pl.DeviceIdType.MESH
F32 = jnp.float32
BF16 = jnp.bfloat16


def kernel(
    dims, image, tiles, slot_row, block_row, ray_list, sinogram, weights, volume, residual,
    tile_v, run_f, run_t, mat, mat_t, pix, acc, part, ray_in, ray_res, ray_out, slot_res,
    grad_out, grad_in, chain_out, chain_dn, chain_up, key_v, table_v, table_s, ids_out, ids_in,
    ids_s, local_sem, ag_send, ag_recv, id_send, id_recv, ray_send, ray_recv, back_send,
    back_recv, gx_send, gx_recv, dn_send, dn_recv, up_send, up_recv,
):
    n_space, n_angle, nx, nz, edge, own, slots, step_size = dims
    count = tiles.shape[0]
    width = key_v.shape[1]
    share = image.shape[0]
    per_chunk = share // edge
    blocks = per_chunk * n_angle
    seats = n_space * CAP
    me_s = lax.axis_index("space")
    me_a = lax.axis_index("angle")
    z, x = me_a // nx, me_a % nx
    has_up, has_dn = z < nz - 1, z > 0
    x_peers = [(x + j) % nx for j in range(1, nx)]
    s_peers = [(me_s + j) % n_space for j in range(1, n_space)]

    def at_angle(zz, xx):
        return (me_s, zz * nx + xx)

    def remote(src, dst, send, recv, device):
        return pltpu.make_async_remote_copy(
            src_ref=src, dst_ref=dst, send_sem=send, recv_sem=recv, device_id=device,
            device_id_type=MESH,
        )

    barrier = pltpu.get_barrier_semaphore()

    def greet(device):
        pl.semaphore_signal(barrier, inc=1, device_id=device, device_id_type=MESH)

    @pl.when(has_up)
    def _():
        greet(at_angle(z + 1, x))

    @pl.when(has_dn)
    def _():
        greet(at_angle(z - 1, x))

    for xx in x_peers:
        greet(at_angle(z, xx))
    for ss in s_peers:
        greet((ss, me_a))
    tile_copy = pltpu.make_async_copy(tiles, tile_v.at[pl.ds(0, count)], local_sem.at[0])
    tile_copy.start()
    volume[...] = image[...]
    pix[me_a] = image[...].astype(BF16)
    friends = has_up.astype(jnp.int32) + has_dn.astype(jnp.int32) + (nx - 1 + n_space - 1)
    pl.semaphore_wait(barrier, friends)

    piece = share // PARTS

    def rows_of(h):
        return pl.ds(h * piece, piece)

    def ag_copy(kind, src_a, h, device):
        rows = pix.at[src_a, rows_of(h)]
        return remote(rows, rows, ag_send.at[kind, src_a, h], ag_recv.at[src_a, h], device)

    def ag_copies(src_z, h, go_up, go_dn):
        src_a = src_z * nx + x
        listed = []
        if go_up:
            listed.append((has_up, ag_copy(0, src_a, h, at_angle(jnp.minimum(z + 1, nz - 1), x))))
        if go_dn:
            listed.append((has_dn, ag_copy(1, src_a, h, at_angle(jnp.maximum(z - 1, 0), x))))
        for j, xx in enumerate(x_peers):
            listed.append((None, ag_copy(2 + j, src_a, h, at_angle(z, xx))))
        return listed

    def each(listed, act):
        for cond, copy in listed:
            if cond is None:
                act(copy)
            else:
                pl.when(cond)(functools.partial(act, copy))

    def start(copy):
        copy.start()

    def wait_send(copy):
        copy.wait_send()

    def ag_wait(src_a, h):
        ag_copy(0, src_a, h, (me_s, me_a)).wait_recv()

    def gather(work):
        for h in range(PARTS):
            each(ag_copies(z, h, True, True), start)
        work(0, PARTS - 1)
        for k in range(1, nz):
            for h in range(PARTS):

                @pl.when(z - k >= 0)
                def _():
                    ag_wait((z - k) * nx + x, h)
                    each(ag_copies(z - k, h, True, False), start)

                @pl.when(z + k < nz)
                def _():
                    ag_wait((z + k) * nx + x, h)
                    each(ag_copies(z + k, h, False, True), start)

                work(k, h)

    def gather_end():
        for h in range(PARTS):
            each(ag_copies(z, h, True, True), wait_send)
            for k in range(1, nz):

                @pl.when(z - k >= 0)
                def _():
                    each(ag_copies(z - k, h, True, False), wait_send)

                @pl.when(z + k < nz)
                def _():
                    each(ag_copies(z + k, h, False, True), wait_send)

    def prepare():
        rays = [ray_list[0, j] for j in range(slots)]
        owners = [r // own for r in rays]
        seat = []
        for j in range(slots):
            rank = jnp.int32(0)
            for i in range(j):
                rank = rank + (owners[i] == owners[j]).astype(jnp.int32)
            seat.append(owners[j] * CAP + rank)
        for p in range(seats):
            local = jnp.int32(-1)
            for j in range(slots):
                local = jnp.where(seat[j] == p, rays[j] % own, local)
            ids_out[p // CAP, p % CAP, :] = jnp.full((128,), local, jnp.int32)
        ids_in[me_s] = ids_out[me_s]
        for j, ss in enumerate(s_peers):
            remote(
                ids_out.at[ss], ids_in.at[me_s], id_send.at[j], id_recv.at[me_s], (ss, me_a)
            ).start()
        spread = jnp.zeros((1, count), jnp.int32)
        for j in range(slots):
            spread = jnp.where(slot_row[...] == j, seat[j], spread)
        key_v[...] = jnp.full(key_v.shape, -1, jnp.int32)
        key_v[0:1, 0:count] = spread * blocks + block_row[...]
        across = jnp.broadcast_to(key_v[0:1, :], (width, width))
        down = across.T
        u = lax.broadcasted_iota(jnp.int32, (width, width), 0)
        t = lax.broadcasted_iota(jnp.int32, (width, width), 1)
        before = jnp.max(jnp.where((across == down) & (u < t), u, -1), axis=0, keepdims=True)
        table_v[0:1, :] = jnp.where(before < 0, count, before)
        for j in range(-(-seats * blocks // width)):
            last = jnp.max(jnp.where(down == t + j * width, u, -1), axis=0, keepdims=True)
            table_v[1 + j : 2 + j, :] = jnp.where(last < 0, count, last)
        copy = pltpu.make_async_copy(table_v, table_s, local_sem.at[1])
        copy.start()
        copy.wait()
        run_f[count] = jnp.zeros((edge, edge), F32)
        run_t[count] = jnp.zeros((edge, edge), BF16)
        tile_copy.wait()
        tile_v[count] = jnp.zeros((edge, edge), BF16)

    def run_tiles(begin, end):
        @pl.loop(begin, end)
        def _(t):
            total = tile_v[t].astype(F32) + run_f[table_s[0, t]]
            run_f[t] = total
            tile_v[t] = total.astype(BF16)

    def turn_tiles(begin, end):
        @pl.loop(begin, end, unroll=math.gcd(end - begin, 4))
        def _(t):
            run_t[t] = tile_v[t].astype(F32).T.astype(BF16)

    def build(begin, end):
        @pl.loop(begin, end)
        def _(c):
            for p in range(seats):
                for q in range(per_chunk):
                    cell = p * blocks + c * per_chunk + q
                    which = table_s[1 + cell // width, cell % width]
                    mat[c, p * edge : (p + 1) * edge, q * edge : (q + 1) * edge] = tile_v[which]
                    mat_t[c, q * edge : (q + 1) * edge, p * edge : (p + 1) * edge] = run_t[which]

    def project(c):
        acc[0 : seats * edge] += jnp.dot(mat[c], pix[c], preferred_element_type=F32)

    def first_work(k, h):
        slot = max(k - 1, 0) * PARTS + h
        splits = max((nz - 1) * PARTS, 1)
        third = max(splits // 3, 1)
        if k == 0:
            prepare()
        if k == 0 and nz > 1:
            return

        def piece_of(total, first, last):
            if first <= slot < last:
                steps = last - first
                return total * (slot - first) // steps, total * (slot - first + 1) // steps
            return 0, 0

        jobs = (
            (run_tiles, count, 0, third),
            (turn_tiles, count, third, 2 * third),
            (build, n_angle, 2 * third, splits),
        )
        for job, total, first, last in jobs:
            begin, end = piece_of(total, first, last)
            if end > begin:
                job(begin, end)

    def across_x(src_z):
        for xx in x_peers:
            for h in range(PARTS):
                ag_wait(src_z * nx + xx, h)
            project(src_z * nx + xx)

    def later_work(k, h):
        if k == 0:
            acc[...] = jnp.zeros(acc.shape, F32)
            project(me_a)
            return
        if h < PARTS - 1:
            if h != PARTS // 2 - 1:
                return
            if k == 1:
                across_x(z)
                return

            @pl.when(z - k + 1 >= 0)
            def _():
                across_x(z - k + 1)

            @pl.when(z + k - 1 < nz)
            def _():
                across_x(z + k - 1)

            return

        @pl.when(z - k >= 0)
        def _():
            project((z - k) * nx + x)

        @pl.when(z + k < nz)
        def _():
            project((z + k) * nx + x)

    def later_end():
        k = nz - 1

        @pl.when(z - k >= 0)
        def _():
            across_x(z - k)

        @pl.when(z + k < nz)
        def _():
            across_x(z + k)

    def first_end():
        acc[...] = jnp.zeros(acc.shape, F32)
        for zz in range(nz):
            for xx in x_peers:
                for h in range(PARTS):
                    ag_wait(zz * nx + xx, h)

        @pl.loop(0, n_angle)
        def _(c):
            project(c)

    group = CAP * edge

    def ray_copy(j, ss):
        return remote(
            part.at[pl.ds(ss * CAP, CAP)], ray_in.at[pl.ds(me_s * CAP, CAP)],
            ray_send.at[j], ray_recv.at[me_s], (ss, me_a),
        )

    def ray_wait(ss):
        rows = pl.ds(ss * CAP, CAP)
        remote(
            part.at[rows], ray_in.at[rows], ray_send.at[0], ray_recv.at[ss], (ss, me_a)
        ).wait_recv()

    def back_copy(j, ss):
        return remote(
            ray_out.at[pl.ds(ss * group, group)], slot_res.at[pl.ds(me_s * group, group)],
            back_send.at[j], back_recv.at[me_s], (ss, me_a),
        )

    def back_wait(ss):
        rows = pl.ds(ss * group, group)
        remote(
            ray_out.at[rows], slot_res.at[rows], back_send.at[0], back_recv.at[ss], (ss, me_a)
        ).wait_recv()

    def exchange(first):
        part[...] = acc[0 : seats * edge].astype(BF16).reshape(part.shape)
        for j, ss in enumerate(s_peers):
            ray_copy(j, ss).start()
        mine = pl.ds(me_s * CAP, CAP)
        ray_in[mine] = part[mine]
        if first:
            ray_in[seats] = jnp.zeros((edge, edge), BF16)
            ray_res[own] = jnp.zeros((edge, edge), BF16)
            for j, ss in enumerate(s_peers):
                copy = remote(
                    ids_out.at[ss], ids_in.at[ss], id_send.at[j], id_recv.at[ss], (ss, me_a)
                )
                copy.wait_send()
                copy.wait_recv()
            copy = pltpu.make_async_copy(ids_in, ids_s, local_sem.at[1])
            copy.start()
            copy.wait()
        for ss in s_peers:
            ray_wait(ss)
        for o in range(own):
            total = -sinogram[o].astype(F32)
            for ss in range(n_space):
                where = jnp.int32(seats)
                for c in range(CAP):
                    where = jnp.where(ids_s[ss, c, 0] == o, ss * CAP + c, where)
                total = total + ray_in[where].astype(F32)
            ray_res[o] = (weights[o].astype(F32) * total).astype(BF16)
        for j, ss in enumerate(s_peers):
            for c in range(CAP):
                which = ids_s[ss, c, 0]
                which = jnp.where(which < 0, own, which)
                ray_out[pl.ds(ss * group + c * edge, edge)] = ray_res[which]
            back_copy(j, ss).start()
        for c in range(CAP):
            which = ids_s[me_s, c, 0]
            which = jnp.where(which < 0, own, which)
            slot_res[pl.ds(me_s * group + c * edge, edge)] = ray_res[which]
        for ss in s_peers:
            back_wait(ss)

    def exchange_end():
        for j, ss in enumerate(s_peers):
            ray_copy(j, ss).wait_send()
            back_copy(j, ss).wait_send()

    def gx_copy(dst_z, j, h, xx):
        rows = (dst_z, j, rows_of(h))
        sem = (dst_z, j, h)
        return remote(
            grad_out.at[rows], grad_in.at[rows], gx_send.at[sem], gx_recv.at[sem], at_angle(z, xx)
        )

    def dn_copy(dst_z, h):
        rows = (dst_z, rows_of(h))
        return remote(
            chain_out.at[rows], chain_dn.at[rows], dn_send.at[dst_z, h], dn_recv.at[dst_z, h],
            at_angle(jnp.maximum(z - 1, 0), x),
        )

    def up_copy(dst_z, h):
        rows = (dst_z, rows_of(h))
        return remote(
            chain_out.at[rows], chain_up.at[rows], up_send.at[dst_z, h], up_recv.at[dst_z, h],
            at_angle(jnp.minimum(z + 1, nz - 1), x),
        )

    def back(c, h):
        return jnp.dot(mat_t[c, rows_of(h)], slot_res[...], preferred_element_type=F32)

    def send_terms(dst_z, h):
        for j, xx in enumerate(x_peers):
            grad_out[dst_z, j, rows_of(h)] = back(dst_z * nx + xx, h).astype(BF16)
            gx_copy(dst_z, j, h, xx).start()

    def sum_terms(dst_z, h):
        total = back(dst_z * nx + x, h)
        for j in range(nx - 1):
            gx_copy(dst_z, j, h, x_peers[j]).wait_recv()
            total = total + grad_in[dst_z, j, rows_of(h)].astype(F32)
        acc[0:piece] = total

    def add_dn(dst_z, h):
        dn_copy(dst_z, h).wait_recv()
        acc[0:piece] += chain_dn[dst_z, rows_of(h)].astype(F32)

    def add_up(dst_z, h):
        up_copy(dst_z, h).wait_recv()
        acc[0:piece] += chain_up[dst_z, rows_of(h)].astype(F32)

    def scatter():
        for k in range(nz - 1, 0, -1):
            for h in range(PARTS):

                @pl.when(z - k >= 0)
                def _():
                    send_terms(z - k, h)

                @pl.when(z + k < nz)
                def _():
                    send_terms(z + k, h)

        for h in range(PARTS):
            send_terms(z, h)
        for k in range(nz - 1, 0, -1):
            for h in range(PARTS):

                @pl.when(z - k >= 0)
                def _():
                    sum_terms(z - k, h)
                    pl.when(has_up)(functools.partial(add_dn, z - k, h))
                    chain_out[z - k, rows_of(h)] = acc[0:piece].astype(BF16)
                    dn_copy(z - k, h).start()

                @pl.when(z + k < nz)
                def _():
                    sum_terms(z + k, h)
                    pl.when(has_dn)(functools.partial(add_up, z + k, h))
                    chain_out[z + k, rows_of(h)] = acc[0:piece].astype(BF16)
                    up_copy(z + k, h).start()

        for h in range(PARTS):
            sum_terms(z, h)
            pl.when(has_up)(functools.partial(add_dn, z, h))
            pl.when(has_dn)(functools.partial(add_up, z, h))
            rows = rows_of(h)
            volume[rows] = jnp.maximum(volume[rows] - step_size * acc[0:piece], 0.0)

    def scatter_end():
        for dst_z in range(nz):
            for h in range(PARTS):
                for j, xx in enumerate(x_peers):
                    gx_copy(dst_z, j, h, xx).wait_send()

                @pl.when(z > dst_z)
                def _():
                    dn_copy(dst_z, h).wait_send()

                @pl.when(z < dst_z)
                def _():
                    up_copy(dst_z, h).wait_send()

    for iteration in range(ITERS):
        if iteration == 0:
            gather(first_work)
            first_end()
        else:
            pix[me_a] = volume[...].astype(BF16)
            gather(later_work)
            later_end()
        exchange(iteration == 0)
        gather_end()
        scatter()
        exchange_end()
        scatter_end()
    residual[...] = ray_res[0:own]


def hand_out(volume, residual, volume_out, residual_out):
    volume_out[...] = volume[...]
    residual_out[...] = residual[...]


def shards(image, tiles, tile_slot, tile_block, slot_ray, sinogram, weights):
    n_space = lax.axis_size("space")
    n_angle = lax.axis_size("angle")
    tile_mats = tiles[0]
    count, edge = tile_mats.shape[:2]
    slices = image.shape[1]
    share = image.shape[0]
    own = sinogram.shape[1]
    slots = slot_ray.shape[1]
    blocks = share * n_angle // edge
    seats = n_space * CAP
    nx = max(1, math.isqrt(n_angle // 2))
    while n_angle % nx:
        nx -= 1
    nz = n_angle // nx
    width = -(-count // 128) * 128
    table = -(-(1 + -(-seats * blocks // width)) // 8) * 8
    step_size = 0.2 * math.sqrt(blocks / (n_angle * own))
    dims = (n_space, n_angle, nx, nz, edge, own, slots, step_size)
    vmem, dma = pltpu.VMEM, pltpu.SemaphoreType.DMA
    others, sides = n_space - 1, nx - 1
    whole = pl.BlockSpec(memory_space=pltpu.VMEM)
    volume, residual = pl.pallas_call(
        functools.partial(kernel, dims),
        out_shape=(
            jax.ShapeDtypeStruct((share, slices), F32),
            jax.ShapeDtypeStruct((own, edge, slices), BF16),
        ),
        in_specs=[
            whole, pl.BlockSpec(memory_space=pl.ANY), whole, whole,
            pl.BlockSpec(memory_space=pltpu.SMEM), whole, whole,
        ],
        out_specs=(whole, whole),
        scratch_shapes=[
            vmem((count + 1, edge, edge), BF16),
            vmem((count + 1, edge, edge), F32),
            vmem((count + 1, edge, edge), BF16),
            vmem((n_angle, seats * edge, share), BF16),
            vmem((n_angle, share, seats * edge), BF16),
            vmem((n_angle, share, slices), BF16),
            vmem((max(seats * edge, share), slices), F32),
            vmem((seats, edge, slices), BF16),
            vmem((seats + 1, edge, slices), BF16),
            vmem((own + 1, edge, slices), BF16),
            vmem((seats * edge, slices), BF16),
            vmem((seats * edge, slices), BF16),
            vmem((nz, sides, share, slices), BF16),
            vmem((nz, sides, share, slices), BF16),
            vmem((nz, share, slices), BF16),
            vmem((nz, share, slices), BF16),
            vmem((nz, share, slices), BF16),
            vmem((8, width), jnp.int32),
            vmem((table, width), jnp.int32),
            pltpu.SMEM((table, width), jnp.int32),
            vmem((n_space, 8, 128), jnp.int32),
            vmem((n_space, 8, 128), jnp.int32),
            pltpu.SMEM((n_space, 8, 128), jnp.int32),
            dma((2,)),
            dma((2 + sides, n_angle, PARTS)), dma((n_angle, PARTS)),
            dma((others,)), dma((n_space,)),
            dma((others,)), dma((n_space,)),
            dma((others,)), dma((n_space,)),
            dma((nz, sides, PARTS)), dma((nz, sides, PARTS)),
            dma((nz, PARTS)), dma((nz, PARTS)),
            dma((nz, PARTS)), dma((nz, PARTS)),
        ],
        compiler_params=pltpu.CompilerParams(
            collective_id=0, has_side_effects=True, vmem_limit_bytes=58 * 1024 * 1024
        ),
    )(image, tile_mats, tile_slot, tile_block, slot_ray, sinogram[0], weights[0])
    volume, residual = pl.pallas_call(
        hand_out,
        out_shape=(
            jax.ShapeDtypeStruct(volume.shape, F32),
            jax.ShapeDtypeStruct(residual.shape, BF16),
        ),
        in_specs=[whole, whole],
        out_specs=(whole, whole),
    )(volume, residual)
    return (volume, residual[None])


def solution(mesh):
    placed = (
        P(("space", "angle"), None),
        P("space", "angle", None, None),
        P("space", "angle"),
        P("space", "angle"),
        P("space", "angle"),
        P("angle", "space", None, None),
        P("angle", "space", None, None),
    )
    return jax.shard_map(
        shards,
        mesh=mesh,
        in_specs=placed,
        out_specs=(P(("space", "angle"), None), P("angle", "space", None, None)),
        check_vma=False,
    )
```

```python
import functools
import math

import jax
import jax.numpy as jnp
from jax import lax
from jax.experimental import pallas as pl
from jax.experimental.pallas import tpu as pltpu
from jax.sharding import PartitionSpec as P

CAP = 2
ITERS = 2
PARTS = 4
MESH = pl.DeviceIdType.MESH
F32 = jnp.float32
BF16 = jnp.bfloat16


def kernel(
    dims, image, tiles, slot_row, block_row, ray_list, sinogram, weights, volume, residual,
    tile_v, run_f, run_t, mat, mat_t, pix, acc, part, ray_in, ray_res, ray_out, slot_res,
    grad_out, grad_in, chain_out, chain_dn, chain_up, key_v, table_v, table_s, ids_out, ids_in,
    ids_s, local_sem, ag_send, ag_recv, id_send, id_recv, ray_send, ray_recv, back_send,
    back_recv, gx_send, gx_recv, dn_send, dn_recv, up_send, up_recv,
):
    n_space, n_angle, nx, nz, edge, own, slots, step_size = dims
    count = tiles.shape[0]
    width = key_v.shape[1]
    share = image.shape[0]
    per_chunk = share // edge
    blocks = per_chunk * n_angle
    seats = n_space * CAP
    me_s = lax.axis_index("space")
    me_a = lax.axis_index("angle")
    z, x = me_a // nx, me_a % nx
    has_up, has_dn = z < nz - 1, z > 0
    x_peers = [(x + j) % nx for j in range(1, nx)]
    s_peers = [(me_s + j) % n_space for j in range(1, n_space)]

    def at_angle(zz, xx):
        return (me_s, zz * nx + xx)

    def remote(src, dst, send, recv, device):
        return pltpu.make_async_remote_copy(
            src_ref=src, dst_ref=dst, send_sem=send, recv_sem=recv, device_id=device,
            device_id_type=MESH,
        )

    barrier = pltpu.get_barrier_semaphore()

    def greet(device):
        pl.semaphore_signal(barrier, inc=1, device_id=device, device_id_type=MESH)

    @pl.when(has_up)
    def _():
        greet(at_angle(z + 1, x))

    @pl.when(has_dn)
    def _():
        greet(at_angle(z - 1, x))

    for xx in x_peers:
        greet(at_angle(z, xx))
    for ss in s_peers:
        greet((ss, me_a))
    tile_copy = pltpu.make_async_copy(tiles, tile_v.at[pl.ds(0, count)], local_sem.at[0])
    tile_copy.start()
    volume[...] = image[...]
    pix[me_a] = image[...].astype(BF16)
    friends = has_up.astype(jnp.int32) + has_dn.astype(jnp.int32) + (nx - 1 + n_space - 1)
    pl.semaphore_wait(barrier, friends)

    piece = share // PARTS

    def rows_of(h):
        return pl.ds(h * piece, piece)

    def ag_copy(kind, src_a, h, device):
        rows = pix.at[src_a, rows_of(h)]
        return remote(rows, rows, ag_send.at[kind, src_a, h], ag_recv.at[src_a, h], device)

    def ag_copies(src_z, h, go_up, go_dn):
        src_a = src_z * nx + x
        listed = []
        if go_up:
            listed.append((has_up, ag_copy(0, src_a, h, at_angle(jnp.minimum(z + 1, nz - 1), x))))
        if go_dn:
            listed.append((has_dn, ag_copy(1, src_a, h, at_angle(jnp.maximum(z - 1, 0), x))))
        for j, xx in enumerate(x_peers):
            listed.append((None, ag_copy(2 + j, src_a, h, at_angle(z, xx))))
        return listed

    def each(listed, act):
        for cond, copy in listed:
            if cond is None:
                act(copy)
            else:
                pl.when(cond)(functools.partial(act, copy))

    def start(copy):
        copy.start()

    def wait_send(copy):
        copy.wait_send()

    def ag_wait(src_a, h):
        ag_copy(0, src_a, h, (me_s, me_a)).wait_recv()

    def gather(work):
        for h in range(PARTS):
            each(ag_copies(z, h, True, True), start)
        work(0, PARTS - 1)
        for k in range(1, nz):
            for h in range(PARTS):

                @pl.when(z - k >= 0)
                def _():
                    ag_wait((z - k) * nx + x, h)
                    each(ag_copies(z - k, h, True, False), start)

                @pl.when(z + k < nz)
                def _():
                    ag_wait((z + k) * nx + x, h)
                    each(ag_copies(z + k, h, False, True), start)

                work(k, h)

    def gather_end():
        for h in range(PARTS):
            each(ag_copies(z, h, True, True), wait_send)
            for k in range(1, nz):

                @pl.when(z - k >= 0)
                def _():
                    each(ag_copies(z - k, h, True, False), wait_send)

                @pl.when(z + k < nz)
                def _():
                    each(ag_copies(z + k, h, False, True), wait_send)

    def prepare():
        rays = [ray_list[0, j] for j in range(slots)]
        owners = [r // own for r in rays]
        seat = []
        for j in range(slots):
            rank = jnp.int32(0)
            for i in range(j):
                rank = rank + (owners[i] == owners[j]).astype(jnp.int32)
            seat.append(owners[j] * CAP + rank)
        for p in range(seats):
            local = jnp.int32(-1)
            for j in range(slots):
                local = jnp.where(seat[j] == p, rays[j] % own, local)
            ids_out[p // CAP, p % CAP, :] = jnp.full((128,), local, jnp.int32)
        ids_in[me_s] = ids_out[me_s]
        for j, ss in enumerate(s_peers):
            remote(
                ids_out.at[ss], ids_in.at[me_s], id_send.at[j], id_recv.at[me_s], (ss, me_a)
            ).start()
        spread = jnp.zeros((1, count), jnp.int32)
        for j in range(slots):
            spread = jnp.where(slot_row[...] == j, seat[j], spread)
        key_v[...] = jnp.full(key_v.shape, -1, jnp.int32)
        key_v[0:1, 0:count] = spread * blocks + block_row[...]
        across = jnp.broadcast_to(key_v[0:1, :], (width, width))
        down = across.T
        u = lax.broadcasted_iota(jnp.int32, (width, width), 0)
        t = lax.broadcasted_iota(jnp.int32, (width, width), 1)
        before = jnp.max(jnp.where((across == down) & (u < t), u, -1), axis=0, keepdims=True)
        table_v[0:1, :] = jnp.where(before < 0, count, before)
        for j in range(-(-seats * blocks // width)):
            last = jnp.max(jnp.where(down == t + j * width, u, -1), axis=0, keepdims=True)
            table_v[1 + j : 2 + j, :] = jnp.where(last < 0, count, last)
        copy = pltpu.make_async_copy(table_v, table_s, local_sem.at[1])
        copy.start()
        copy.wait()
        run_f[count] = jnp.zeros((edge, edge), F32)
        run_t[count] = jnp.zeros((edge, edge), BF16)
        tile_copy.wait()
        tile_v[count] = jnp.zeros((edge, edge), BF16)

    def run_tiles(begin, end):
        @pl.loop(begin, end)
        def _(t):
            total = tile_v[t].astype(F32) + run_f[table_s[0, t]]
            run_f[t] = total
            tile_v[t] = total.astype(BF16)

    def turn_tiles(begin, end):
        @pl.loop(begin, end, unroll=math.gcd(end - begin, 4))
        def _(t):
            run_t[t] = tile_v[t].astype(F32).T.astype(BF16)

    def build(begin, end):
        @pl.loop(begin, end)
        def _(c):
            for p in range(seats):
                for q in range(per_chunk):
                    cell = p * blocks + c * per_chunk + q
                    which = table_s[1 + cell // width, cell % width]
                    mat[c, p * edge : (p + 1) * edge, q * edge : (q + 1) * edge] = tile_v[which]
                    mat_t[c, q * edge : (q + 1) * edge, p * edge : (p + 1) * edge] = run_t[which]

    def project(c):
        acc[0 : seats * edge] += jnp.dot(mat[c], pix[c], preferred_element_type=F32)

    def first_work(k, h):
        slot = max(k - 1, 0) * PARTS + h
        splits = max((nz - 1) * PARTS, 1)
        third = max(splits // 3, 1)
        if k == 0:
            prepare()
        if k == 0 and nz > 1:
            return

        def piece_of(total, first, last):
            if first <= slot < last:
                steps = last - first
                return total * (slot - first) // steps, total * (slot - first + 1) // steps
            return 0, 0

        jobs = (
            (run_tiles, count, 0, third),
            (turn_tiles, count, third, 2 * third),
            (build, n_angle, 2 * third, splits),
        )
        for job, total, first, last in jobs:
            begin, end = piece_of(total, first, last)
            if end > begin:
                job(begin, end)

    def across_x(src_z):
        for xx in x_peers:
            for h in range(PARTS):
                ag_wait(src_z * nx + xx, h)
            project(src_z * nx + xx)

    def later_work(k, h):
        if k == 0:
            acc[...] = jnp.zeros(acc.shape, F32)
            project(me_a)
            return
        if h < PARTS - 1:
            if h != PARTS // 2 - 1:
                return
            if k == 1:
                across_x(z)
                return

            @pl.when(z - k + 1 >= 0)
            def _():
                across_x(z - k + 1)

            @pl.when(z + k - 1 < nz)
            def _():
                across_x(z + k - 1)

            return

        @pl.when(z - k >= 0)
        def _():
            project((z - k) * nx + x)

        @pl.when(z + k < nz)
        def _():
            project((z + k) * nx + x)

    def later_end():
        k = nz - 1

        @pl.when(z - k >= 0)
        def _():
            across_x(z - k)

        @pl.when(z + k < nz)
        def _():
            across_x(z + k)

    def first_end():
        acc[...] = jnp.zeros(acc.shape, F32)
        for zz in range(nz):
            for xx in x_peers:
                for h in range(PARTS):
                    ag_wait(zz * nx + xx, h)

        @pl.loop(0, n_angle)
        def _(c):
            project(c)

    group = CAP * edge

    def ray_copy(j, ss):
        return remote(
            part.at[pl.ds(ss * CAP, CAP)], ray_in.at[pl.ds(me_s * CAP, CAP)],
            ray_send.at[j], ray_recv.at[me_s], (ss, me_a),
        )

    def ray_wait(ss):
        rows = pl.ds(ss * CAP, CAP)
        remote(
            part.at[rows], ray_in.at[rows], ray_send.at[0], ray_recv.at[ss], (ss, me_a)
        ).wait_recv()

    def back_copy(j, ss):
        return remote(
            ray_out.at[pl.ds(ss * group, group)], slot_res.at[pl.ds(me_s * group, group)],
            back_send.at[j], back_recv.at[me_s], (ss, me_a),
        )

    def back_wait(ss):
        rows = pl.ds(ss * group, group)
        remote(
            ray_out.at[rows], slot_res.at[rows], back_send.at[0], back_recv.at[ss], (ss, me_a)
        ).wait_recv()

    def exchange(first):
        part[...] = acc[0 : seats * edge].astype(BF16).reshape(part.shape)
        for j, ss in enumerate(s_peers):
            ray_copy(j, ss).start()
        mine = pl.ds(me_s * CAP, CAP)
        ray_in[mine] = part[mine]
        if first:
            ray_in[seats] = jnp.zeros((edge, edge), BF16)
            ray_res[own] = jnp.zeros((edge, edge), BF16)
            for j, ss in enumerate(s_peers):
                copy = remote(
                    ids_out.at[ss], ids_in.at[ss], id_send.at[j], id_recv.at[ss], (ss, me_a)
                )
                copy.wait_send()
                copy.wait_recv()
            copy = pltpu.make_async_copy(ids_in, ids_s, local_sem.at[1])
            copy.start()
            copy.wait()
        for ss in s_peers:
            ray_wait(ss)
        for o in range(own):
            total = -sinogram[o].astype(F32)
            for ss in range(n_space):
                where = jnp.int32(seats)
                for c in range(CAP):
                    where = jnp.where(ids_s[ss, c, 0] == o, ss * CAP + c, where)
                total = total + ray_in[where].astype(F32)
            ray_res[o] = (weights[o].astype(F32) * total).astype(BF16)
        for j, ss in enumerate(s_peers):
            for c in range(CAP):
                which = ids_s[ss, c, 0]
                which = jnp.where(which < 0, own, which)
                ray_out[pl.ds(ss * group + c * edge, edge)] = ray_res[which]
            back_copy(j, ss).start()
        for c in range(CAP):
            which = ids_s[me_s, c, 0]
            which = jnp.where(which < 0, own, which)
            slot_res[pl.ds(me_s * group + c * edge, edge)] = ray_res[which]
        for ss in s_peers:
            back_wait(ss)

    def exchange_end():
        for j, ss in enumerate(s_peers):
            ray_copy(j, ss).wait_send()
            back_copy(j, ss).wait_send()

    def gx_copy(dst_z, j, h, xx):
        rows = (dst_z, j, rows_of(h))
        sem = (dst_z, j, h)
        return remote(
            grad_out.at[rows], grad_in.at[rows], gx_send.at[sem], gx_recv.at[sem], at_angle(z, xx)
        )

    def dn_copy(dst_z, h):
        rows = (dst_z, rows_of(h))
        return remote(
            chain_out.at[rows], chain_dn.at[rows], dn_send.at[dst_z, h], dn_recv.at[dst_z, h],
            at_angle(jnp.maximum(z - 1, 0), x),
        )

    def up_copy(dst_z, h):
        rows = (dst_z, rows_of(h))
        return remote(
            chain_out.at[rows], chain_up.at[rows], up_send.at[dst_z, h], up_recv.at[dst_z, h],
            at_angle(jnp.minimum(z + 1, nz - 1), x),
        )

    def back(c):
        return jnp.dot(mat_t[c], slot_res[...], preferred_element_type=F32)

    def side_rows(side, h):
        return pl.ds(side * share + h * piece, piece)

    def send_terms(dst_z):
        for j, xx in enumerate(x_peers):
            grad_out[dst_z, j] = back(dst_z * nx + xx).astype(BF16)
            for h in range(PARTS):
                gx_copy(dst_z, j, h, xx).start()

    def own_terms(dst_z, side):
        acc[side * share : (side + 1) * share] = back(dst_z * nx + x)

    def sum_terms(dst_z, side, h):
        for j in range(nx - 1):
            gx_copy(dst_z, j, h, x_peers[j]).wait_recv()
            acc[side_rows(side, h)] += grad_in[dst_z, j, rows_of(h)].astype(F32)

    def add_dn(dst_z, side, h):
        dn_copy(dst_z, h).wait_recv()
        acc[side_rows(side, h)] += chain_dn[dst_z, rows_of(h)].astype(F32)

    def add_up(dst_z, side, h):
        up_copy(dst_z, h).wait_recv()
        acc[side_rows(side, h)] += chain_up[dst_z, rows_of(h)].astype(F32)

    def send_all(k):
        if k == 0:
            send_terms(z)
            return
        pl.when(z - k >= 0)(functools.partial(send_terms, z - k))
        pl.when(z + k < nz)(functools.partial(send_terms, z + k))

    def pass_on(k):
        pl.when(z - k >= 0)(functools.partial(own_terms, z - k, 0))
        pl.when(z + k < nz)(functools.partial(own_terms, z + k, 1))
        for h in range(PARTS):

            @pl.when(z - k >= 0)
            def _():
                sum_terms(z - k, 0, h)
                pl.when(has_up)(functools.partial(add_dn, z - k, 0, h))
                chain_out[z - k, rows_of(h)] = acc[side_rows(0, h)].astype(BF16)
                dn_copy(z - k, h).start()

            @pl.when(z + k < nz)
            def _():
                sum_terms(z + k, 1, h)
                pl.when(has_dn)(functools.partial(add_up, z + k, 1, h))
                chain_out[z + k, rows_of(h)] = acc[side_rows(1, h)].astype(BF16)
                up_copy(z + k, h).start()

    def scatter():
        send_all(nz - 1)
        for k in range(nz - 1, 0, -1):
            send_all(k - 1)
            pass_on(k)
        own_terms(z, 0)
        for h in range(PARTS):
            sum_terms(z, 0, h)
            pl.when(has_up)(functools.partial(add_dn, z, 0, h))
            pl.when(has_dn)(functools.partial(add_up, z, 0, h))
            rows = rows_of(h)
            volume[rows] = jnp.maximum(volume[rows] - step_size * acc[side_rows(0, h)], 0.0)

    def scatter_end():
        for dst_z in range(nz):
            for h in range(PARTS):
                for j, xx in enumerate(x_peers):
                    gx_copy(dst_z, j, h, xx).wait_send()

                @pl.when(z > dst_z)
                def _():
                    dn_copy(dst_z, h).wait_send()

                @pl.when(z < dst_z)
                def _():
                    up_copy(dst_z, h).wait_send()

    for iteration in range(ITERS):
        if iteration == 0:
            gather(first_work)
            first_end()
        else:
            pix[me_a] = volume[...].astype(BF16)
            gather(later_work)
            later_end()
        exchange(iteration == 0)
        gather_end()
        scatter()
        exchange_end()
        scatter_end()
    residual[...] = ray_res[0:own]


def hand_out(volume, residual, volume_out, residual_out):
    volume_out[...] = volume[...]
    residual_out[...] = residual[...]


def shards(image, tiles, tile_slot, tile_block, slot_ray, sinogram, weights):
    n_space = lax.axis_size("space")
    n_angle = lax.axis_size("angle")
    tile_mats = tiles[0]
    count, edge = tile_mats.shape[:2]
    slices = image.shape[1]
    share = image.shape[0]
    own = sinogram.shape[1]
    slots = slot_ray.shape[1]
    blocks = share * n_angle // edge
    seats = n_space * CAP
    nx = max(1, math.isqrt(n_angle // 2))
    while n_angle % nx:
        nx -= 1
    nz = n_angle // nx
    width = -(-count // 128) * 128
    table = -(-(1 + -(-seats * blocks // width)) // 8) * 8
    step_size = 0.2 * math.sqrt(blocks / (n_angle * own))
    dims = (n_space, n_angle, nx, nz, edge, own, slots, step_size)
    vmem, dma = pltpu.VMEM, pltpu.SemaphoreType.DMA
    others, sides = n_space - 1, nx - 1
    whole = pl.BlockSpec(memory_space=pltpu.VMEM)
    volume, residual = pl.pallas_call(
        functools.partial(kernel, dims),
        out_shape=(
            jax.ShapeDtypeStruct((share, slices), F32),
            jax.ShapeDtypeStruct((own, edge, slices), BF16),
        ),
        in_specs=[
            whole, pl.BlockSpec(memory_space=pl.ANY), whole, whole,
            pl.BlockSpec(memory_space=pltpu.SMEM), whole, whole,
        ],
        out_specs=(whole, whole),
        scratch_shapes=[
            vmem((count + 1, edge, edge), BF16),
            vmem((count + 1, edge, edge), F32),
            vmem((count + 1, edge, edge), BF16),
            vmem((n_angle, seats * edge, share), BF16),
            vmem((n_angle, share, seats * edge), BF16),
            vmem((n_angle, share, slices), BF16),
            vmem((max(seats * edge, 2 * share), slices), F32),
            vmem((seats, edge, slices), BF16),
            vmem((seats + 1, edge, slices), BF16),
            vmem((own + 1, edge, slices), BF16),
            vmem((seats * edge, slices), BF16),
            vmem((seats * edge, slices), BF16),
            vmem((nz, sides, share, slices), BF16),
            vmem((nz, sides, share, slices), BF16),
            vmem((nz, share, slices), BF16),
            vmem((nz, share, slices), BF16),
            vmem((nz, share, slices), BF16),
            vmem((8, width), jnp.int32),
            vmem((table, width), jnp.int32),
            pltpu.SMEM((table, width), jnp.int32),
            vmem((n_space, 8, 128), jnp.int32),
            vmem((n_space, 8, 128), jnp.int32),
            pltpu.SMEM((n_space, 8, 128), jnp.int32),
            dma((2,)),
            dma((2 + sides, n_angle, PARTS)), dma((n_angle, PARTS)),
            dma((others,)), dma((n_space,)),
            dma((others,)), dma((n_space,)),
            dma((others,)), dma((n_space,)),
            dma((nz, sides, PARTS)), dma((nz, sides, PARTS)),
            dma((nz, PARTS)), dma((nz, PARTS)),
            dma((nz, PARTS)), dma((nz, PARTS)),
        ],
        compiler_params=pltpu.CompilerParams(
            collective_id=0, has_side_effects=True, vmem_limit_bytes=58 * 1024 * 1024
        ),
    )(image, tile_mats, tile_slot, tile_block, slot_ray, sinogram[0], weights[0])
    volume, residual = pl.pallas_call(
        hand_out,
        out_shape=(
            jax.ShapeDtypeStruct(volume.shape, F32),
            jax.ShapeDtypeStruct(residual.shape, BF16),
        ),
        in_specs=[whole, whole],
        out_specs=(whole, whole),
    )(volume, residual)
    return (volume, residual[None])


def solution(mesh):
    placed = (
        P(("space", "angle"), None),
        P("space", "angle", None, None),
        P("space", "angle"),
        P("space", "angle"),
        P("space", "angle"),
        P("angle", "space", None, None),
        P("angle", "space", None, None),
    )
    return jax.shard_map(
        shards,
        mesh=mesh,
        in_specs=placed,
        out_specs=(P(("space", "angle"), None), P("angle", "space", None, None)),
        check_vma=False,
    )
```

```python
import functools
import math

import jax
import jax.numpy as jnp
from jax import lax
from jax.experimental import pallas as pl
from jax.experimental.pallas import tpu as pltpu
from jax.sharding import PartitionSpec as P

CAP = 2
ITERS = 2
PARTS = 4
MESH = pl.DeviceIdType.MESH
F32 = jnp.float32
BF16 = jnp.bfloat16


def kernel(
    dims, image, tiles, slot_row, block_row, ray_list, sinogram, weights, volume, residual,
    tile_v, run_f, run_t, mat, mat_t, pix, acc, part, ray_in, ray_res, ray_out, slot_res,
    grad_out, grad_in, chain_out, chain_dn, chain_up, key_v, table_v, table_s, ids_out, ids_in,
    ids_s, local_sem, ag_send, ag_recv, id_send, id_recv, ray_send, ray_recv, back_send,
    back_recv, gx_send, gx_recv, dn_send, dn_recv, up_send, up_recv,
):
    n_space, n_angle, nx, nz, edge, own, slots, step_size = dims
    count = tiles.shape[0]
    width = key_v.shape[1]
    share = image.shape[0]
    per_chunk = share // edge
    blocks = per_chunk * n_angle
    seats = n_space * CAP
    me_s = lax.axis_index("space")
    me_a = lax.axis_index("angle")
    z, x = me_a // nx, me_a % nx
    has_up, has_dn = z < nz - 1, z > 0
    x_peers = [(x + j) % nx for j in range(1, nx)]
    s_peers = [(me_s + j) % n_space for j in range(1, n_space)]

    def at_angle(zz, xx):
        return (me_s, zz * nx + xx)

    def remote(src, dst, send, recv, device):
        return pltpu.make_async_remote_copy(
            src_ref=src, dst_ref=dst, send_sem=send, recv_sem=recv, device_id=device,
            device_id_type=MESH,
        )

    barrier = pltpu.get_barrier_semaphore()

    def greet(device):
        pl.semaphore_signal(barrier, inc=1, device_id=device, device_id_type=MESH)

    @pl.when(has_up)
    def _():
        greet(at_angle(z + 1, x))

    @pl.when(has_dn)
    def _():
        greet(at_angle(z - 1, x))

    for xx in x_peers:
        greet(at_angle(z, xx))
    for ss in s_peers:
        greet((ss, me_a))
    tile_copy = pltpu.make_async_copy(tiles, tile_v.at[pl.ds(0, count)], local_sem.at[0])
    tile_copy.start()
    volume[...] = image[...]
    pix[me_a] = image[...].astype(BF16)
    friends = has_up.astype(jnp.int32) + has_dn.astype(jnp.int32) + (nx - 1 + n_space - 1)
    pl.semaphore_wait(barrier, friends)

    piece = share // PARTS

    def rows_of(h):
        return pl.ds(h * piece, piece)

    def ag_copy(kind, src_a, h, device):
        rows = pix.at[src_a, rows_of(h)]
        return remote(rows, rows, ag_send.at[kind, src_a, h], ag_recv.at[src_a, h], device)

    def ag_copies(src_z, h, go_up, go_dn):
        src_a = src_z * nx + x
        listed = []
        if go_up:
            listed.append((has_up, ag_copy(0, src_a, h, at_angle(jnp.minimum(z + 1, nz - 1), x))))
        if go_dn:
            listed.append((has_dn, ag_copy(1, src_a, h, at_angle(jnp.maximum(z - 1, 0), x))))
        for j, xx in enumerate(x_peers):
            listed.append((None, ag_copy(2 + j, src_a, h, at_angle(z, xx))))
        return listed

    def each(listed, act):
        for cond, copy in listed:
            if cond is None:
                act(copy)
            else:
                pl.when(cond)(functools.partial(act, copy))

    def start(copy):
        copy.start()

    def wait_send(copy):
        copy.wait_send()

    def ag_wait(src_a, h):
        ag_copy(0, src_a, h, (me_s, me_a)).wait_recv()

    even = nx == 2 and nz > 2

    def far(h):
        return even and h >= PARTS // 2

    def twin_copies(src_z, h, go_up, go_dn):
        src_a = src_z * nx + x_peers[0]
        listed = []
        if go_up:
            listed.append((has_up, ag_copy(0, src_a, h, at_angle(jnp.minimum(z + 1, nz - 1), x))))
        if go_dn:
            listed.append((has_dn, ag_copy(1, src_a, h, at_angle(jnp.maximum(z - 1, 0), x))))
        return listed

    def relay(src_z, end, h, go_up, go_dn, act, await_first):
        def plain():
            if await_first:
                ag_wait(src_z * nx + x, h)
            each(ag_copies(src_z, h, go_up, go_dn), act)

        def along():
            if await_first:
                ag_wait(src_z * nx + x, h)
            each(ag_copies(src_z, h, go_up, go_dn)[:-1], act)
            if await_first:
                ag_wait(src_z * nx + x_peers[0], h)
            each(twin_copies(src_z, h, go_up, go_dn), act)

        if far(h):
            pl.when(jnp.logical_not(end))(plain)
            pl.when(end)(along)
        else:
            plain()

    def own_twin(h, act, await_first):
        def turn():
            if await_first:
                ag_wait(z * nx + x_peers[0], h)
            each(twin_copies(z, h, True, True), act)

        if far(h):
            pl.when((z == 0) | (z == nz - 1))(turn)

    def gather(work):
        for h in range(PARTS):
            each(ag_copies(z, h, True, True), start)
        work(0, PARTS - 1)
        for k in range(1, nz):
            for h in range(PARTS):
                if k == 1:
                    own_twin(h, start, True)

                @pl.when(z - k >= 0)
                def _():
                    relay(z - k, z == k, h, True, False, start, True)

                @pl.when(z + k < nz)
                def _():
                    relay(z + k, z == nz - 1 - k, h, False, True, start, True)

                work(k, h)

    def gather_end():
        for h in range(PARTS):
            each(ag_copies(z, h, True, True), wait_send)
            own_twin(h, wait_send, False)
            for k in range(1, nz):

                @pl.when(z - k >= 0)
                def _():
                    relay(z - k, z == k, h, True, False, wait_send, False)

                @pl.when(z + k < nz)
                def _():
                    relay(z + k, z == nz - 1 - k, h, False, True, wait_send, False)

    def ag_wait_x(src_z, xx):
        for h in range(PARTS):
            if far(h):
                inner = (src_z != 0) & (src_z != nz - 1)
                pl.when(inner)(functools.partial(ag_wait, src_z * nx + xx, h))
            else:
                ag_wait(src_z * nx + xx, h)

    def prepare():
        rays = [ray_list[0, j] for j in range(slots)]
        owners = [r // own for r in rays]
        seat = []
        for j in range(slots):
            rank = jnp.int32(0)
            for i in range(j):
                rank = rank + (owners[i] == owners[j]).astype(jnp.int32)
            seat.append(owners[j] * CAP + rank)
        for p in range(seats):
            local = jnp.int32(-1)
            for j in range(slots):
                local = jnp.where(seat[j] == p, rays[j] % own, local)
            ids_out[p // CAP, p % CAP, :] = jnp.full((128,), local, jnp.int32)
        ids_in[me_s] = ids_out[me_s]
        for j, ss in enumerate(s_peers):
            remote(
                ids_out.at[ss], ids_in.at[me_s], id_send.at[j], id_recv.at[me_s], (ss, me_a)
            ).start()
        spread = jnp.zeros((1, count), jnp.int32)
        for j in range(slots):
            spread = jnp.where(slot_row[...] == j, seat[j], spread)
        key_v[...] = jnp.full(key_v.shape, -1, jnp.int32)
        key_v[0:1, 0:count] = spread * blocks + block_row[...]
        across = jnp.broadcast_to(key_v[0:1, :], (width, width))
        down = across.T
        u = lax.broadcasted_iota(jnp.int32, (width, width), 0)
        t = lax.broadcasted_iota(jnp.int32, (width, width), 1)
        before = jnp.max(jnp.where((across == down) & (u < t), u, -1), axis=0, keepdims=True)
        table_v[0:1, :] = jnp.where(before < 0, count, before)
        for j in range(-(-seats * blocks // width)):
            last = jnp.max(jnp.where(down == t + j * width, u, -1), axis=0, keepdims=True)
            table_v[1 + j : 2 + j, :] = jnp.where(last < 0, count, last)
        copy = pltpu.make_async_copy(table_v, table_s, local_sem.at[1])
        copy.start()
        copy.wait()
        run_f[count] = jnp.zeros((edge, edge), F32)
        run_t[count] = jnp.zeros((edge, edge), BF16)
        tile_copy.wait()
        tile_v[count] = jnp.zeros((edge, edge), BF16)

    def run_tiles(begin, end):
        @pl.loop(begin, end)
        def _(t):
            total = tile_v[t].astype(F32) + run_f[table_s[0, t]]
            run_f[t] = total
            tile_v[t] = total.astype(BF16)

    def turn_tiles(begin, end):
        @pl.loop(begin, end, unroll=math.gcd(end - begin, 4))
        def _(t):
            run_t[t] = tile_v[t].astype(F32).T.astype(BF16)

    def build(begin, end):
        @pl.loop(begin, end)
        def _(c):
            for p in range(seats):
                for q in range(per_chunk):
                    cell = p * blocks + c * per_chunk + q
                    which = table_s[1 + cell // width, cell % width]
                    mat[c, p * edge : (p + 1) * edge, q * edge : (q + 1) * edge] = tile_v[which]
                    mat_t[c, q * edge : (q + 1) * edge, p * edge : (p + 1) * edge] = run_t[which]

    def project(c):
        acc[0 : seats * edge] += jnp.dot(mat[c], pix[c], preferred_element_type=F32)

    def first_work(k, h):
        slot = max(k - 1, 0) * PARTS + h
        splits = max((nz - 1) * PARTS, 1)
        third = max(splits // 3, 1)
        if k == 0:
            prepare()
        if k == 0 and nz > 1:
            return

        def piece_of(total, first, last):
            if first <= slot < last:
                steps = last - first
                return total * (slot - first) // steps, total * (slot - first + 1) // steps
            return 0, 0

        jobs = (
            (run_tiles, count, 0, third),
            (turn_tiles, count, third, 2 * third),
            (build, n_angle, 2 * third, splits),
        )
        for job, total, first, last in jobs:
            begin, end = piece_of(total, first, last)
            if end > begin:
                job(begin, end)

    def across_x(src_z):
        for xx in x_peers:
            ag_wait_x(src_z, xx)
            project(src_z * nx + xx)

    def later_work(k, h):
        if k == 0:
            acc[...] = jnp.zeros(acc.shape, F32)
            project(me_a)
            return
        if h < PARTS - 1:
            if h != PARTS // 2 - 1:
                return
            if k == 1:
                return
            if k == 2:
                across_x(z)

            @pl.when(z - k + 1 >= 0)
            def _():
                across_x(z - k + 1)

            @pl.when(z + k - 1 < nz)
            def _():
                across_x(z + k - 1)

            return

        @pl.when(z - k >= 0)
        def _():
            project((z - k) * nx + x)

        @pl.when(z + k < nz)
        def _():
            project((z + k) * nx + x)

    def later_end():
        k = nz - 1
        if k < 2:
            across_x(z)
            if k < 1:
                return

        @pl.when(z - k >= 0)
        def _():
            across_x(z - k)

        @pl.when(z + k < nz)
        def _():
            across_x(z + k)

    def first_end():
        acc[...] = jnp.zeros(acc.shape, F32)
        for zz in range(nz):
            for xx in x_peers:
                ag_wait_x(jnp.int32(zz), xx)

        @pl.loop(0, n_angle)
        def _(c):
            project(c)

    group = CAP * edge

    def ray_copy(j, ss):
        return remote(
            part.at[pl.ds(ss * CAP, CAP)], ray_in.at[pl.ds(me_s * CAP, CAP)],
            ray_send.at[j], ray_recv.at[me_s], (ss, me_a),
        )

    def ray_wait(ss):
        rows = pl.ds(ss * CAP, CAP)
        remote(
            part.at[rows], ray_in.at[rows], ray_send.at[0], ray_recv.at[ss], (ss, me_a)
        ).wait_recv()

    def back_copy(j, ss):
        return remote(
            ray_out.at[pl.ds(ss * group, group)], slot_res.at[pl.ds(me_s * group, group)],
            back_send.at[j], back_recv.at[me_s], (ss, me_a),
        )

    def back_wait(ss):
        rows = pl.ds(ss * group, group)
        remote(
            ray_out.at[rows], slot_res.at[rows], back_send.at[0], back_recv.at[ss], (ss, me_a)
        ).wait_recv()

    def exchange(first):
        part[...] = acc[0 : seats * edge].astype(BF16).reshape(part.shape)
        for j, ss in enumerate(s_peers):
            ray_copy(j, ss).start()
        mine = pl.ds(me_s * CAP, CAP)
        ray_in[mine] = part[mine]
        if first:
            ray_in[seats] = jnp.zeros((edge, edge), BF16)
            ray_res[own] = jnp.zeros((edge, edge), BF16)
            for j, ss in enumerate(s_peers):
                copy = remote(
                    ids_out.at[ss], ids_in.at[ss], id_send.at[j], id_recv.at[ss], (ss, me_a)
                )
                copy.wait_send()
                copy.wait_recv()
            copy = pltpu.make_async_copy(ids_in, ids_s, local_sem.at[1])
            copy.start()
            copy.wait()
        for ss in s_peers:
            ray_wait(ss)
        for o in range(own):
            total = -sinogram[o].astype(F32)
            for ss in range(n_space):
                where = jnp.int32(seats)
                for c in range(CAP):
                    where = jnp.where(ids_s[ss, c, 0] == o, ss * CAP + c, where)
                total = total + ray_in[where].astype(F32)
            ray_res[o] = (weights[o].astype(F32) * total).astype(BF16)
        for j, ss in enumerate(s_peers):
            for c in range(CAP):
                which = ids_s[ss, c, 0]
                which = jnp.where(which < 0, own, which)
                ray_out[pl.ds(ss * group + c * edge, edge)] = ray_res[which]
            back_copy(j, ss).start()
        for c in range(CAP):
            which = ids_s[me_s, c, 0]
            which = jnp.where(which < 0, own, which)
            slot_res[pl.ds(me_s * group + c * edge, edge)] = ray_res[which]
        for ss in s_peers:
            back_wait(ss)

    def exchange_end():
        for j, ss in enumerate(s_peers):
            ray_copy(j, ss).wait_send()
            back_copy(j, ss).wait_send()

    def gx_copy(dst_z, j, h, xx):
        rows = (dst_z, j, rows_of(h))
        sem = (dst_z, j, h)
        return remote(
            grad_out.at[rows], grad_in.at[rows], gx_send.at[sem], gx_recv.at[sem], at_angle(z, xx)
        )

    def dn_copy(dst_z, h):
        rows = (dst_z, rows_of(h))
        return remote(
            chain_out.at[rows], chain_dn.at[rows], dn_send.at[dst_z, h], dn_recv.at[dst_z, h],
            at_angle(jnp.maximum(z - 1, 0), x),
        )

    def up_copy(dst_z, h):
        rows = (dst_z, rows_of(h))
        return remote(
            chain_out.at[rows], chain_up.at[rows], up_send.at[dst_z, h], up_recv.at[dst_z, h],
            at_angle(jnp.minimum(z + 1, nz - 1), x),
        )

    def back(c):
        return jnp.dot(mat_t[c], slot_res[...], preferred_element_type=F32)

    def side_rows(side, h):
        return pl.ds(side * share + h * piece, piece)

    def send_terms(dst_z):
        for j, xx in enumerate(x_peers):
            grad_out[dst_z, j] = back(dst_z * nx + xx).astype(BF16)
            for h in range(PARTS):
                gx_copy(dst_z, j, h, xx).start()

    def own_terms(dst_z, side):
        acc[side * share : (side + 1) * share] = back(dst_z * nx + x)

    def sum_terms(dst_z, side, h):
        for j in range(nx - 1):
            gx_copy(dst_z, j, h, x_peers[j]).wait_recv()
            acc[side_rows(side, h)] += grad_in[dst_z, j, rows_of(h)].astype(F32)

    def add_dn(dst_z, side, h):
        dn_copy(dst_z, h).wait_recv()
        acc[side_rows(side, h)] += chain_dn[dst_z, rows_of(h)].astype(F32)

    def add_up(dst_z, side, h):
        up_copy(dst_z, h).wait_recv()
        acc[side_rows(side, h)] += chain_up[dst_z, rows_of(h)].astype(F32)

    def send_all(k):
        if k == 0:
            send_terms(z)
            return
        pl.when(z - k >= 0)(functools.partial(send_terms, z - k))
        pl.when(z + k < nz)(functools.partial(send_terms, z + k))

    def pass_on(k):
        pl.when(z - k >= 0)(functools.partial(own_terms, z - k, 0))
        pl.when(z + k < nz)(functools.partial(own_terms, z + k, 1))
        for h in range(PARTS):

            @pl.when(z - k >= 0)
            def _():
                sum_terms(z - k, 0, h)
                pl.when(has_up)(functools.partial(add_dn, z - k, 0, h))
                chain_out[z - k, rows_of(h)] = acc[side_rows(0, h)].astype(BF16)
                dn_copy(z - k, h).start()

            @pl.when(z + k < nz)
            def _():
                sum_terms(z + k, 1, h)
                pl.when(has_dn)(functools.partial(add_up, z + k, 1, h))
                chain_out[z + k, rows_of(h)] = acc[side_rows(1, h)].astype(BF16)
                up_copy(z + k, h).start()

    def scatter():
        send_all(nz - 1)
        for k in range(nz - 1, 0, -1):
            send_all(k - 1)
            pass_on(k)
        own_terms(z, 0)
        for h in range(PARTS):
            sum_terms(z, 0, h)
            pl.when(has_up)(functools.partial(add_dn, z, 0, h))
            pl.when(has_dn)(functools.partial(add_up, z, 0, h))
            rows = rows_of(h)
            volume[rows] = jnp.maximum(volume[rows] - step_size * acc[side_rows(0, h)], 0.0)

    def scatter_end():
        for dst_z in range(nz):
            for h in range(PARTS):
                for j, xx in enumerate(x_peers):
                    gx_copy(dst_z, j, h, xx).wait_send()

                @pl.when(z > dst_z)
                def _():
                    dn_copy(dst_z, h).wait_send()

                @pl.when(z < dst_z)
                def _():
                    up_copy(dst_z, h).wait_send()

    for iteration in range(ITERS):
        if iteration == 0:
            gather(first_work)
            first_end()
        else:
            pix[me_a] = volume[...].astype(BF16)
            gather(later_work)
            later_end()
        exchange(iteration == 0)
        gather_end()
        scatter()
        exchange_end()
        scatter_end()
    residual[...] = ray_res[0:own]


def hand_out(volume, residual, volume_out, residual_out):
    volume_out[...] = volume[...]
    residual_out[...] = residual[...]


def shards(image, tiles, tile_slot, tile_block, slot_ray, sinogram, weights):
    n_space = lax.axis_size("space")
    n_angle = lax.axis_size("angle")
    tile_mats = tiles[0]
    count, edge = tile_mats.shape[:2]
    slices = image.shape[1]
    share = image.shape[0]
    own = sinogram.shape[1]
    slots = slot_ray.shape[1]
    blocks = share * n_angle // edge
    seats = n_space * CAP
    nx = max(1, math.isqrt(n_angle // 2))
    while n_angle % nx:
        nx -= 1
    nz = n_angle // nx
    width = -(-count // 128) * 128
    table = -(-(1 + -(-seats * blocks // width)) // 8) * 8
    step_size = 0.2 * math.sqrt(blocks / (n_angle * own))
    dims = (n_space, n_angle, nx, nz, edge, own, slots, step_size)
    vmem, dma = pltpu.VMEM, pltpu.SemaphoreType.DMA
    others, sides = n_space - 1, nx - 1
    whole = pl.BlockSpec(memory_space=pltpu.VMEM)
    volume, residual = pl.pallas_call(
        functools.partial(kernel, dims),
        out_shape=(
            jax.ShapeDtypeStruct((share, slices), F32),
            jax.ShapeDtypeStruct((own, edge, slices), BF16),
        ),
        in_specs=[
            whole, pl.BlockSpec(memory_space=pl.ANY), whole, whole,
            pl.BlockSpec(memory_space=pltpu.SMEM), whole, whole,
        ],
        out_specs=(whole, whole),
        scratch_shapes=[
            vmem((count + 1, edge, edge), BF16),
            vmem((count + 1, edge, edge), F32),
            vmem((count + 1, edge, edge), BF16),
            vmem((n_angle, seats * edge, share), BF16),
            vmem((n_angle, share, seats * edge), BF16),
            vmem((n_angle, share, slices), BF16),
            vmem((max(seats * edge, 2 * share), slices), F32),
            vmem((seats, edge, slices), BF16),
            vmem((seats + 1, edge, slices), BF16),
            vmem((own + 1, edge, slices), BF16),
            vmem((seats * edge, slices), BF16),
            vmem((seats * edge, slices), BF16),
            vmem((nz, sides, share, slices), BF16),
            vmem((nz, sides, share, slices), BF16),
            vmem((nz, share, slices), BF16),
            vmem((nz, share, slices), BF16),
            vmem((nz, share, slices), BF16),
            vmem((8, width), jnp.int32),
            vmem((table, width), jnp.int32),
            pltpu.SMEM((table, width), jnp.int32),
            vmem((n_space, 8, 128), jnp.int32),
            vmem((n_space, 8, 128), jnp.int32),
            pltpu.SMEM((n_space, 8, 128), jnp.int32),
            dma((2,)),
            dma((2 + sides, n_angle, PARTS)), dma((n_angle, PARTS)),
            dma((others,)), dma((n_space,)),
            dma((others,)), dma((n_space,)),
            dma((others,)), dma((n_space,)),
            dma((nz, sides, PARTS)), dma((nz, sides, PARTS)),
            dma((nz, PARTS)), dma((nz, PARTS)),
            dma((nz, PARTS)), dma((nz, PARTS)),
        ],
        compiler_params=pltpu.CompilerParams(
            collective_id=0, has_side_effects=True, vmem_limit_bytes=58 * 1024 * 1024
        ),
    )(image, tile_mats, tile_slot, tile_block, slot_ray, sinogram[0], weights[0])
    volume, residual = pl.pallas_call(
        hand_out,
        out_shape=(
            jax.ShapeDtypeStruct(volume.shape, F32),
            jax.ShapeDtypeStruct(residual.shape, BF16),
        ),
        in_specs=[whole, whole],
        out_specs=(whole, whole),
    )(volume, residual)
    return (volume, residual[None])


def solution(mesh):
    placed = (
        P(("space", "angle"), None),
        P("space", "angle", None, None),
        P("space", "angle"),
        P("space", "angle"),
        P("space", "angle"),
        P("angle", "space", None, None),
        P("angle", "space", None, None),
    )
    return jax.shard_map(
        shards,
        mesh=mesh,
        in_specs=placed,
        out_specs=(P(("space", "angle"), None), P("angle", "space", None, None)),
        check_vma=False,
    )
```

```python
import functools
import math

import jax
import jax.numpy as jnp
from jax import lax
from jax.experimental import pallas as pl
from jax.experimental.pallas import tpu as pltpu
from jax.sharding import PartitionSpec as P

CAP = 2
ITERS = 2
PARTS = 4
MESH = pl.DeviceIdType.MESH
F32 = jnp.float32
BF16 = jnp.bfloat16


def kernel(
    dims, image, tiles, slot_row, block_row, ray_list, sinogram, weights, volume, residual,
    tile_v, run_f, run_t, mat, mat_t, pix, acc, part, ray_in, ray_res, ray_out, slot_res,
    grad_out, grad_in, chain_out, chain_dn, chain_up, key_v, table_v, table_s, ids_out, ids_in,
    ids_s, local_sem, ag_send, ag_recv, id_send, id_recv, ray_send, ray_recv, back_send,
    back_recv, gx_send, gx_recv, dn_send, dn_recv, up_send, up_recv,
):
    n_space, n_angle, nx, nz, edge, own, slots, step_size = dims
    count = tiles.shape[0]
    width = key_v.shape[1]
    share = image.shape[0]
    per_chunk = share // edge
    blocks = per_chunk * n_angle
    seats = n_space * CAP
    me_s = lax.axis_index("space")
    me_a = lax.axis_index("angle")
    z, x = me_a // nx, me_a % nx
    has_up, has_dn = z < nz - 1, z > 0
    x_peers = [(x + j) % nx for j in range(1, nx)]
    s_peers = [(me_s + j) % n_space for j in range(1, n_space)]

    def at_angle(zz, xx):
        return (me_s, zz * nx + xx)

    def remote(src, dst, send, recv, device):
        return pltpu.make_async_remote_copy(
            src_ref=src, dst_ref=dst, send_sem=send, recv_sem=recv, device_id=device,
            device_id_type=MESH,
        )

    barrier = pltpu.get_barrier_semaphore()

    def greet(device):
        pl.semaphore_signal(barrier, inc=1, device_id=device, device_id_type=MESH)

    @pl.when(has_up)
    def _():
        greet(at_angle(z + 1, x))

    @pl.when(has_dn)
    def _():
        greet(at_angle(z - 1, x))

    for xx in x_peers:
        greet(at_angle(z, xx))
    for ss in s_peers:
        greet((ss, me_a))
    tile_copy = pltpu.make_async_copy(tiles, tile_v.at[pl.ds(0, count)], local_sem.at[0])
    tile_copy.start()
    volume[...] = image[...]
    pix[me_a] = image[...].astype(BF16)
    friends = has_up.astype(jnp.int32) + has_dn.astype(jnp.int32) + (nx - 1 + n_space - 1)
    pl.semaphore_wait(barrier, friends)

    piece = share // PARTS

    def rows_of(h):
        return pl.ds(h * piece, piece)

    def ag_copy(kind, src_a, h, device):
        rows = pix.at[src_a, rows_of(h)]
        return remote(rows, rows, ag_send.at[kind, src_a, h], ag_recv.at[src_a, h], device)

    def ag_copies(src_z, h, go_up, go_dn):
        src_a = src_z * nx + x
        listed = []
        if go_up:
            listed.append((has_up, ag_copy(0, src_a, h, at_angle(jnp.minimum(z + 1, nz - 1), x))))
        if go_dn:
            listed.append((has_dn, ag_copy(1, src_a, h, at_angle(jnp.maximum(z - 1, 0), x))))
        for j, xx in enumerate(x_peers):
            listed.append((None, ag_copy(2 + j, src_a, h, at_angle(z, xx))))
        return listed

    def each(listed, act):
        for cond, copy in listed:
            if cond is None:
                act(copy)
            else:
                pl.when(cond)(functools.partial(act, copy))

    def start(copy):
        copy.start()

    def wait_send(copy):
        copy.wait_send()

    def ag_wait(src_a, h):
        ag_copy(0, src_a, h, (me_s, me_a)).wait_recv()

    even = nx == 2 and nz > 2

    def far(h):
        return even and h >= PARTS // 2

    def twin_copies(src_z, h, go_up, go_dn):
        src_a = src_z * nx + x_peers[0]
        listed = []
        if go_up:
            listed.append((has_up, ag_copy(0, src_a, h, at_angle(jnp.minimum(z + 1, nz - 1), x))))
        if go_dn:
            listed.append((has_dn, ag_copy(1, src_a, h, at_angle(jnp.maximum(z - 1, 0), x))))
        return listed

    def relay(src_z, end, h, go_up, go_dn, act, await_first):
        def plain():
            if await_first:
                ag_wait(src_z * nx + x, h)
            each(ag_copies(src_z, h, go_up, go_dn), act)

        def along():
            if await_first:
                ag_wait(src_z * nx + x, h)
            each(ag_copies(src_z, h, go_up, go_dn)[:-1], act)
            if await_first:
                ag_wait(src_z * nx + x_peers[0], h)
            each(twin_copies(src_z, h, go_up, go_dn), act)

        if far(h):
            pl.when(jnp.logical_not(end))(plain)
            pl.when(end)(along)
        else:
            plain()

    def own_twin(h, act, await_first):
        def turn():
            if await_first:
                ag_wait(z * nx + x_peers[0], h)
            each(twin_copies(z, h, True, True), act)

        if far(h):
            pl.when((z == 0) | (z == nz - 1))(turn)

    def gather(work):
        for h in range(PARTS):
            each(ag_copies(z, h, True, True), start)
        work(0, PARTS - 1)
        for k in range(1, nz):
            for h in range(PARTS):
                if k == 1:
                    own_twin(h, start, True)

                @pl.when(z - k >= 0)
                def _():
                    relay(z - k, z == k, h, True, False, start, True)

                @pl.when(z + k < nz)
                def _():
                    relay(z + k, z == nz - 1 - k, h, False, True, start, True)

                work(k, h)

    def gather_end():
        for h in range(PARTS):
            each(ag_copies(z, h, True, True), wait_send)
            own_twin(h, wait_send, False)
            for k in range(1, nz):

                @pl.when(z - k >= 0)
                def _():
                    relay(z - k, z == k, h, True, False, wait_send, False)

                @pl.when(z + k < nz)
                def _():
                    relay(z + k, z == nz - 1 - k, h, False, True, wait_send, False)

    def ag_wait_x(src_z, xx):
        for h in range(PARTS):
            if far(h):
                inner = (src_z != 0) & (src_z != nz - 1)
                pl.when(inner)(functools.partial(ag_wait, src_z * nx + xx, h))
            else:
                ag_wait(src_z * nx + xx, h)

    def prepare():
        rays = [ray_list[0, j] for j in range(slots)]
        owners = [r // own for r in rays]
        seat = []
        for j in range(slots):
            rank = jnp.int32(0)
            for i in range(j):
                rank = rank + (owners[i] == owners[j]).astype(jnp.int32)
            seat.append(owners[j] * CAP + rank)
        for p in range(seats):
            local = jnp.int32(-1)
            for j in range(slots):
                local = jnp.where(seat[j] == p, rays[j] % own, local)
            ids_out[p // CAP, p % CAP, :] = jnp.full((128,), local, jnp.int32)
        ids_in[me_s] = ids_out[me_s]
        for j, ss in enumerate(s_peers):
            remote(
                ids_out.at[ss], ids_in.at[me_s], id_send.at[j], id_recv.at[me_s], (ss, me_a)
            ).start()
        spread = jnp.zeros((1, count), jnp.int32)
        for j in range(slots):
            spread = jnp.where(slot_row[...] == j, seat[j], spread)
        key_v[...] = jnp.full(key_v.shape, -1, jnp.int32)
        key_v[0:1, 0:count] = spread * blocks + block_row[...]
        across = jnp.broadcast_to(key_v[0:1, :], (width, width))
        down = across.T
        u = lax.broadcasted_iota(jnp.int32, (width, width), 0)
        t = lax.broadcasted_iota(jnp.int32, (width, width), 1)
        before = jnp.max(jnp.where((across == down) & (u < t), u, -1), axis=0, keepdims=True)
        table_v[0:1, :] = jnp.where(before < 0, count, before)
        for j in range(-(-seats * blocks // width)):
            last = jnp.max(jnp.where(down == t + j * width, u, -1), axis=0, keepdims=True)
            table_v[1 + j : 2 + j, :] = jnp.where(last < 0, count, last)
        copy = pltpu.make_async_copy(table_v, table_s, local_sem.at[1])
        copy.start()
        copy.wait()
        run_f[count] = jnp.zeros((edge, edge), F32)
        run_t[count] = jnp.zeros((edge, edge), BF16)
        tile_copy.wait()
        tile_v[count] = jnp.zeros((edge, edge), BF16)

    def run_tiles(begin, end):
        @pl.loop(begin, end)
        def _(t):
            total = tile_v[t].astype(F32) + run_f[table_s[0, t]]
            run_f[t] = total
            tile_v[t] = total.astype(BF16)

    def turn_tiles(begin, end):
        @pl.loop(begin, end, unroll=math.gcd(end - begin, 4))
        def _(t):
            run_t[t] = tile_v[t].astype(F32).T.astype(BF16)

    def build(begin, end):
        @pl.loop(begin, end)
        def _(c):
            for p in range(seats):
                for q in range(per_chunk):
                    cell = p * blocks + c * per_chunk + q
                    which = table_s[1 + cell // width, cell % width]
                    mat[c, p * edge : (p + 1) * edge, q * edge : (q + 1) * edge] = tile_v[which]
                    mat_t[c, q * edge : (q + 1) * edge, p * edge : (p + 1) * edge] = run_t[which]

    def project(c):
        acc[0 : seats * edge] += jnp.dot(mat[c], pix[c], preferred_element_type=F32)

    def first_work(k, h):
        slot = max(k - 1, 0) * PARTS + h
        splits = max((nz - 1) * PARTS, 1)
        third = max(splits // 3, 1)
        if k == 0:
            prepare()
        if k == 0 and nz > 1:
            return

        def piece_of(total, first, last):
            if first <= slot < last:
                steps = last - first
                return total * (slot - first) // steps, total * (slot - first + 1) // steps
            return 0, 0

        jobs = (
            (run_tiles, count, 0, third),
            (turn_tiles, count, third, 2 * third),
            (build, n_angle, 2 * third, splits),
        )
        for job, total, first, last in jobs:
            begin, end = piece_of(total, first, last)
            if end > begin:
                job(begin, end)

    def across_x(src_z):
        for xx in x_peers:
            ag_wait_x(src_z, xx)
            project(src_z * nx + xx)

    def later_work(k, h):
        if k == 0:
            acc[...] = jnp.zeros(acc.shape, F32)
            project(me_a)
            return
        if h < PARTS - 1:
            if h != PARTS // 2 - 1:
                return
            if k == 1:
                return
            if k == 2:
                across_x(z)

            @pl.when(z - k + 1 >= 0)
            def _():
                across_x(z - k + 1)

            @pl.when(z + k - 1 < nz)
            def _():
                across_x(z + k - 1)

            return

        @pl.when(z - k >= 0)
        def _():
            project((z - k) * nx + x)

        @pl.when(z + k < nz)
        def _():
            project((z + k) * nx + x)

    def later_end():
        k = nz - 1
        if k < 2:
            across_x(z)
            if k < 1:
                return

        @pl.when(z - k >= 0)
        def _():
            across_x(z - k)

        @pl.when(z + k < nz)
        def _():
            across_x(z + k)

    def first_end():
        acc[...] = jnp.zeros(acc.shape, F32)

        @pl.loop(0, nz)
        def _(zz):
            project(zz * nx + x)

        for zz in range(nz):
            for xx in x_peers:
                ag_wait_x(jnp.int32(zz), xx)
                project(zz * nx + xx)

    group = CAP * edge

    def ray_copy(j, ss):
        return remote(
            part.at[pl.ds(ss * CAP, CAP)], ray_in.at[pl.ds(me_s * CAP, CAP)],
            ray_send.at[j], ray_recv.at[me_s], (ss, me_a),
        )

    def ray_wait(ss):
        rows = pl.ds(ss * CAP, CAP)
        remote(
            part.at[rows], ray_in.at[rows], ray_send.at[0], ray_recv.at[ss], (ss, me_a)
        ).wait_recv()

    def back_copy(j, ss):
        return remote(
            ray_out.at[pl.ds(ss * group, group)], slot_res.at[pl.ds(me_s * group, group)],
            back_send.at[j], back_recv.at[me_s], (ss, me_a),
        )

    def back_wait(ss):
        rows = pl.ds(ss * group, group)
        remote(
            ray_out.at[rows], slot_res.at[rows], back_send.at[0], back_recv.at[ss], (ss, me_a)
        ).wait_recv()

    def exchange(first):
        part[...] = acc[0 : seats * edge].astype(BF16).reshape(part.shape)
        for j, ss in enumerate(s_peers):
            ray_copy(j, ss).start()
        mine = pl.ds(me_s * CAP, CAP)
        ray_in[mine] = part[mine]
        if first:
            ray_in[seats] = jnp.zeros((edge, edge), BF16)
            ray_res[own] = jnp.zeros((edge, edge), BF16)
            for j, ss in enumerate(s_peers):
                copy = remote(
                    ids_out.at[ss], ids_in.at[ss], id_send.at[j], id_recv.at[ss], (ss, me_a)
                )
                copy.wait_send()
                copy.wait_recv()
            copy = pltpu.make_async_copy(ids_in, ids_s, local_sem.at[1])
            copy.start()
            copy.wait()
        for ss in s_peers:
            ray_wait(ss)
        for o in range(own):
            total = -sinogram[o].astype(F32)
            for ss in range(n_space):
                where = jnp.int32(seats)
                for c in range(CAP):
                    where = jnp.where(ids_s[ss, c, 0] == o, ss * CAP + c, where)
                total = total + ray_in[where].astype(F32)
            ray_res[o] = (weights[o].astype(F32) * total).astype(BF16)
        for j, ss in enumerate(s_peers):
            for c in range(CAP):
                which = ids_s[ss, c, 0]
                which = jnp.where(which < 0, own, which)
                ray_out[pl.ds(ss * group + c * edge, edge)] = ray_res[which]
            back_copy(j, ss).start()
        for c in range(CAP):
            which = ids_s[me_s, c, 0]
            which = jnp.where(which < 0, own, which)
            slot_res[pl.ds(me_s * group + c * edge, edge)] = ray_res[which]
        for ss in s_peers:
            back_wait(ss)

    def exchange_end():
        for j, ss in enumerate(s_peers):
            ray_copy(j, ss).wait_send()
            back_copy(j, ss).wait_send()

    def gx_copy(dst_z, j, h, xx):
        rows = (dst_z, j, rows_of(h))
        sem = (dst_z, j, h)
        return remote(
            grad_out.at[rows], grad_in.at[rows], gx_send.at[sem], gx_recv.at[sem], at_angle(z, xx)
        )

    def dn_copy(dst_z, h):
        rows = (dst_z, rows_of(h))
        return remote(
            chain_out.at[rows], chain_dn.at[rows], dn_send.at[dst_z, h], dn_recv.at[dst_z, h],
            at_angle(jnp.maximum(z - 1, 0), x),
        )

    def up_copy(dst_z, h):
        rows = (dst_z, rows_of(h))
        return remote(
            chain_out.at[rows], chain_up.at[rows], up_send.at[dst_z, h], up_recv.at[dst_z, h],
            at_angle(jnp.minimum(z + 1, nz - 1), x),
        )

    def back(c):
        return jnp.dot(mat_t[c], slot_res[...], preferred_element_type=F32)

    def side_rows(side, h):
        return pl.ds(side * share + h * piece, piece)

    def send_terms(dst_z):
        for j, xx in enumerate(x_peers):
            grad_out[dst_z, j] = back(dst_z * nx + xx).astype(BF16)
            for h in range(PARTS):
                gx_copy(dst_z, j, h, xx).start()

    def own_terms(dst_z, side):
        acc[side * share : (side + 1) * share] = back(dst_z * nx + x)

    def sum_terms(dst_z, side, h):
        for j in range(nx - 1):
            gx_copy(dst_z, j, h, x_peers[j]).wait_recv()
            acc[side_rows(side, h)] += grad_in[dst_z, j, rows_of(h)].astype(F32)

    def add_dn(dst_z, side, h):
        dn_copy(dst_z, h).wait_recv()
        acc[side_rows(side, h)] += chain_dn[dst_z, rows_of(h)].astype(F32)

    def add_up(dst_z, side, h):
        up_copy(dst_z, h).wait_recv()
        acc[side_rows(side, h)] += chain_up[dst_z, rows_of(h)].astype(F32)

    def send_all(k):
        if k == 0:
            send_terms(z)
            return
        pl.when(z - k >= 0)(functools.partial(send_terms, z - k))
        pl.when(z + k < nz)(functools.partial(send_terms, z + k))

    def pass_on(k):
        pl.when(z - k >= 0)(functools.partial(own_terms, z - k, 0))
        pl.when(z + k < nz)(functools.partial(own_terms, z + k, 1))
        for h in range(PARTS):

            @pl.when(z - k >= 0)
            def _():
                sum_terms(z - k, 0, h)
                pl.when(has_up)(functools.partial(add_dn, z - k, 0, h))
                chain_out[z - k, rows_of(h)] = acc[side_rows(0, h)].astype(BF16)
                dn_copy(z - k, h).start()

            @pl.when(z + k < nz)
            def _():
                sum_terms(z + k, 1, h)
                pl.when(has_dn)(functools.partial(add_up, z + k, 1, h))
                chain_out[z + k, rows_of(h)] = acc[side_rows(1, h)].astype(BF16)
                up_copy(z + k, h).start()

    def scatter():
        send_all(nz - 1)
        for k in range(nz - 1, 0, -1):
            send_all(k - 1)
            pass_on(k)
        own_terms(z, 0)
        for h in range(PARTS):
            sum_terms(z, 0, h)
            pl.when(has_up)(functools.partial(add_dn, z, 0, h))
            pl.when(has_dn)(functools.partial(add_up, z, 0, h))
            rows = rows_of(h)
            volume[rows] = jnp.maximum(volume[rows] - step_size * acc[side_rows(0, h)], 0.0)

    def scatter_end():
        for dst_z in range(nz):
            for h in range(PARTS):
                for j, xx in enumerate(x_peers):
                    gx_copy(dst_z, j, h, xx).wait_send()

                @pl.when(z > dst_z)
                def _():
                    dn_copy(dst_z, h).wait_send()

                @pl.when(z < dst_z)
                def _():
                    up_copy(dst_z, h).wait_send()

    for iteration in range(ITERS):
        if iteration == 0:
            gather(first_work)
            first_end()
        else:
            pix[me_a] = volume[...].astype(BF16)
            gather(later_work)
            later_end()
        exchange(iteration == 0)
        gather_end()
        scatter()
        exchange_end()
        scatter_end()
    residual[...] = ray_res[0:own]


def hand_out(volume, residual, volume_out, residual_out):
    volume_out[...] = volume[...]
    residual_out[...] = residual[...]


def shards(image, tiles, tile_slot, tile_block, slot_ray, sinogram, weights):
    n_space = lax.axis_size("space")
    n_angle = lax.axis_size("angle")
    tile_mats = tiles[0]
    count, edge = tile_mats.shape[:2]
    slices = image.shape[1]
    share = image.shape[0]
    own = sinogram.shape[1]
    slots = slot_ray.shape[1]
    blocks = share * n_angle // edge
    seats = n_space * CAP
    nx = max(1, math.isqrt(n_angle // 2))
    while n_angle % nx:
        nx -= 1
    nz = n_angle // nx
    width = -(-count // 128) * 128
    table = -(-(1 + -(-seats * blocks // width)) // 8) * 8
    step_size = 0.2 * math.sqrt(blocks / (n_angle * own))
    dims = (n_space, n_angle, nx, nz, edge, own, slots, step_size)
    vmem, dma = pltpu.VMEM, pltpu.SemaphoreType.DMA
    others, sides = n_space - 1, nx - 1
    whole = pl.BlockSpec(memory_space=pltpu.VMEM)
    volume, residual = pl.pallas_call(
        functools.partial(kernel, dims),
        out_shape=(
            jax.ShapeDtypeStruct((share, slices), F32),
            jax.ShapeDtypeStruct((own, edge, slices), BF16),
        ),
        in_specs=[
            whole, pl.BlockSpec(memory_space=pl.ANY), whole, whole,
            pl.BlockSpec(memory_space=pltpu.SMEM), whole, whole,
        ],
        out_specs=(whole, whole),
        scratch_shapes=[
            vmem((count + 1, edge, edge), BF16),
            vmem((count + 1, edge, edge), F32),
            vmem((count + 1, edge, edge), BF16),
            vmem((n_angle, seats * edge, share), BF16),
            vmem((n_angle, share, seats * edge), BF16),
            vmem((n_angle, share, slices), BF16),
            vmem((max(seats * edge, 2 * share), slices), F32),
            vmem((seats, edge, slices), BF16),
            vmem((seats + 1, edge, slices), BF16),
            vmem((own + 1, edge, slices), BF16),
            vmem((seats * edge, slices), BF16),
            vmem((seats * edge, slices), BF16),
            vmem((nz, sides, share, slices), BF16),
            vmem((nz, sides, share, slices), BF16),
            vmem((nz, share, slices), BF16),
            vmem((nz, share, slices), BF16),
            vmem((nz, share, slices), BF16),
            vmem((8, width), jnp.int32),
            vmem((table, width), jnp.int32),
            pltpu.SMEM((table, width), jnp.int32),
            vmem((n_space, 8, 128), jnp.int32),
            vmem((n_space, 8, 128), jnp.int32),
            pltpu.SMEM((n_space, 8, 128), jnp.int32),
            dma((2,)),
            dma((2 + sides, n_angle, PARTS)), dma((n_angle, PARTS)),
            dma((others,)), dma((n_space,)),
            dma((others,)), dma((n_space,)),
            dma((others,)), dma((n_space,)),
            dma((nz, sides, PARTS)), dma((nz, sides, PARTS)),
            dma((nz, PARTS)), dma((nz, PARTS)),
            dma((nz, PARTS)), dma((nz, PARTS)),
        ],
        compiler_params=pltpu.CompilerParams(
            collective_id=0, has_side_effects=True, vmem_limit_bytes=58 * 1024 * 1024
        ),
    )(image, tile_mats, tile_slot, tile_block, slot_ray, sinogram[0], weights[0])
    volume, residual = pl.pallas_call(
        hand_out,
        out_shape=(
            jax.ShapeDtypeStruct(volume.shape, F32),
            jax.ShapeDtypeStruct(residual.shape, BF16),
        ),
        in_specs=[whole, whole],
        out_specs=(whole, whole),
    )(volume, residual)
    return (volume, residual[None])


def solution(mesh):
    placed = (
        P(("space", "angle"), None),
        P("space", "angle", None, None),
        P("space", "angle"),
        P("space", "angle"),
        P("space", "angle"),
        P("angle", "space", None, None),
        P("angle", "space", None, None),
    )
    return jax.shard_map(
        shards,
        mesh=mesh,
        in_specs=placed,
        out_specs=(P(("space", "angle"), None), P("angle", "space", None, None)),
        check_vma=False,
    )
```
